32 devices in a mesh: ref: 2 (over x), dp: 16 (over z, y, core).
Axes of the slice: x: 2, y: 2, z: 4, core: 2. Of those that a mesh axis runs over, the one named last changes fastest.
Arguments:
- particles: bfloat16 [32, 64, 4096], P(('ref', 'dp')), may hold values from -8 to 8
- references: bfloat16 [2, 64, 4096], P(None, 'dp'), may hold values from -6 to 6
- orient: int32 [16, 6], replicated, may hold values from 0 to 2, as said below
- allowed: int32 [32, 2], P(('ref', 'dp')), may hold values from 0 to 1, as said below
Outputs:
- sums: float32 [16, 64, 4096], P('ref', 'dp')
- log_evidence: float32 [32], P(('ref', 'dp'))
The draws below stay inside these ranges and needn't reach their ends.
Inputs may be any that keep to these rules, and one draw needn't show every extreme that they name: `orient`: the first three entries of each row are a permutation of 0, 1, 2; the last three are 0 or 1. Every particle has at least one allowed class.
All inputs are finite; a program needn't handle non-finite values.
Results may differ from the reference program's by a relative error of at most 0.0027.
Values may be sent and summed in bfloat16 or wider, within the bound.
No kernel may reach another device: no remote copies, remote signals or barrier semaphores. Data moves between devices by JAX's collectives and lax.ppermute only.
A program may use at most 128 MiB of HBM per device.

```python
import math
import jax
import jax.numpy as jnp
from jax import lax

N = 64
CLS = 2
ORI = 8
PARTICLES = 32


def one_order(subkey):
    return jax.random.permutation(subkey, 3)


def shared_orient(key):
    key = jax.random.fold_in(key, 311)
    subkeys = jax.random.split(key, CLS * ORI)
    orders = jax.vmap(one_order)(subkeys).astype(jnp.int32)
    flips = jax.random.randint(jax.random.fold_in(key, 5), (CLS * ORI, 3), 0, 2).astype(jnp.int32)
    return jnp.concatenate([orders, flips], axis=1)


def shared_references(key):
    key = jax.random.fold_in(key, 321)
    return jnp.clip(jax.random.normal(key, (CLS, N, N, N), jnp.float32), -6.0, 6.0)


def shared_picks(key):
    key = jax.random.fold_in(key, 331)
    return jax.random.randint(key, (PARTICLES,), 0, CLS).astype(jnp.int32)


def draw_orient(key, part):
    return shared_orient(key)


def draw_references(key, part):
    return shared_references(key).reshape(CLS, N, N * N).astype(jnp.bfloat16)


def draw_allowed(key, part):
    picks = shared_picks(key)
    key = jax.random.fold_in(key, 23)
    base = jax.random.randint(key, (PARTICLES, CLS), 0, 2)
    forced = (jnp.arange(CLS, dtype=jnp.int32)[None, :] == picks[:, None]).astype(jnp.int32)
    return jnp.maximum(base, forced).astype(jnp.int32)


def draw_particles(key, part):
    key = jax.random.fold_in(key, 41)
    return jnp.clip(jax.random.normal(key, (PARTICLES, N, N * N), jnp.float32), -6.0, 6.0).astype(jnp.bfloat16)


def setup_inputs(seed: int = 0) -> dict:
    keys = jax.random.split(jax.random.key(seed), 5)
    particles = draw_particles(jax.random.fold_in(keys[4], 71), 0)
    references = draw_references(jax.random.fold_in(keys[4], 71), 0)
    orient = draw_orient(jax.random.fold_in(keys[4], 71), 0)
    allowed = draw_allowed(jax.random.fold_in(keys[4], 71), 0)
    return {"particles": particles, "references": references, "orient": orient, "allowed": allowed}


MOVES = [(0, 0, 0), (1, 0, 0), (-1, 0, 0), (0, 1, 0), (0, -1, 0), (0, 0, 1), (0, 0, -1)]

def rotate(volume, code):
    edge = volume.shape[0]
    line = jnp.arange(edge, dtype=jnp.int32)
    coords = [line[:, None, None], line[None, :, None], line[None, None, :]]
    strides = jnp.array([edge * edge, edge, 1], dtype=jnp.int32)
    flat = jnp.zeros((edge, edge, edge), jnp.int32)
    for axis in range(3):
        source = coords[axis] + code[3 + axis] * (edge - 1 - 2 * coords[axis])
        flat = flat + source * strides[code[axis]]
    return volume.reshape(-1)[flat.reshape(-1)].reshape(edge, edge, edge)

def reference(particles, references, orient, allowed):
    count, edge = (particles.shape[0], particles.shape[1])
    voxels = edge ** 3
    cubes = particles.reshape(count, edge, edge, edge)
    classes = jnp.arange(orient.shape[0], dtype=jnp.int32) // ORI
    volumes = references.reshape(references.shape[0], edge, edge, edge)
    rotated = jax.vmap(rotate)(volumes[classes], orient).reshape(orient.shape[0], voxels)
    scale = 3.0 / math.sqrt(voxels)
    logits = []
    for move in MOVES:
        shifted = jnp.roll(cubes, (-move[0], -move[1], -move[2]), axis=(1, 2, 3)).reshape(count, voxels)
        logits.append(jnp.dot(shifted, rotated.T, preferred_element_type=jnp.float32) * scale)
    logits = jnp.stack(logits)
    permit = jnp.take(allowed, classes, axis=1)[None] == 1
    logits = jnp.where(permit, logits, jnp.float32(-1e+30))
    top = lax.optimization_barrier(jnp.max(logits, axis=(0, 2)))
    expo = jnp.exp(logits - top[None, :, None])
    total = lax.optimization_barrier(jnp.sum(expo, axis=(0, 2)))
    weights = (expo / total[None, :, None]).astype(jnp.bfloat16)
    log_evidence = top + jnp.log(total)
    sums = jnp.zeros((orient.shape[0], voxels), jnp.float32)
    for index in range(len(MOVES)):
        move = MOVES[index]
        shifted = jnp.roll(cubes, (-move[0], -move[1], -move[2]), axis=(1, 2, 3)).reshape(count, voxels)
        sums = sums + jnp.dot(weights[index].T, shifted, preferred_element_type=jnp.float32)
    return (sums.reshape(orient.shape[0], edge, edge * edge), log_evidence)
```

```python
import functools
import math

import jax
import jax.numpy as jnp
from jax import lax
from jax.experimental import pallas as pl
from jax.experimental.pallas import tpu as pltpu
from jax.sharding import PartitionSpec as P

ORI = 8
LANES = 128
ROWS = 8
MOVES = [(0, 0, 0), (1, 0, 0), (-1, 0, 0), (0, 1, 0), (0, -1, 0), (0, 0, 1), (0, 0, -1)]
FLAT = [(0, 0), (1, 0), (-1, 0), (0, 1), (0, -1)]
SLOTS = 8
BARRED = -1e30
VMEM_BYTES = 48 * 1024 * 1024


def lane_iota(shape):
    return lax.broadcasted_iota(jnp.int32, shape, len(shape) - 1)


def swap_halves(x):
    return pltpu.roll(x, LANES // 2, 1)


def transpose_planes(source, target, planes, edge):
    for n in range(0, planes, 2):
        turned = source[n * edge : (n + 2) * edge, :].T[:edge, :]
        target[n * edge : (n + 1) * edge, :] = turned
        target[(n + 1) * edge : (n + 2) * edge, :] = swap_halves(turned)


def flatten_planes(source, planes, edge, store):
    low = lane_iota((planes, LANES)) < edge
    for m in range(edge // 2):
        even = source[pl.ds(2 * m, planes, stride=edge), :]
        odd = source[pl.ds(2 * m + 1, planes, stride=edge), :]
        store(m, jnp.where(low, even, swap_halves(odd)))


def pack_kernel(edge, parts, part_ref, refs_ref, out_ref, both_ref, ring, stage, x, z, flat, turned):
    h = edge // parts
    planes = 2 * h
    wide = edge * edge
    spare = ROWS - h - 2
    span = 4 * h * edge
    ring[ROWS : ROWS + edge, :] = part_ref[...].astype(jnp.float32)
    ring[ROWS - 1 : ROWS, :] = ring[ROWS + edge - 1 : ROWS + edge, :]
    ring[ROWS + edge : ROWS + edge + 1, :] = ring[ROWS : ROWS + 1, :]
    for c in range(2):
        x[c * h : (c + 1) * h, :] = refs_ref[c].astype(jnp.float32)
    for m in range(edge // 2):
        piece = x[:planes, m * LANES : (m + 1) * LANES]
        flat[pl.ds(2 * m, planes, stride=edge), :] = piece
        flat[pl.ds(2 * m + 1, planes, stride=edge), :] = swap_halves(piece)
    transpose_planes(flat, turned, planes, edge)

    def store(m, value):
        z[:planes, m * LANES : (m + 1) * LANES] = value

    flatten_planes(turned, planes, edge, store)
    if planes // spare * span < wide:
        stage[...] = jnp.zeros_like(stage)
    slab = h * edge
    for s in range(parts):
        top = s * ROWS
        stage[top : top + h + 2, :] = ring[ROWS + h * s - 1 : ROWS + h * s + h + 1, :]
        mirror = parts - 1 - s
        for q in range(planes // spare):
            rows = slice(q * spare, (q + 1) * spare)
            for number, (array, place) in enumerate(((x, s), (x, mirror), (z, s), (z, mirror))):
                left = q * span + number * slab
                stage[top + h + 2 : top + ROWS, left : left + slab] = array[rows, place * slab : (place + 1) * slab]
    out_ref[...] = stage[...].astype(jnp.bfloat16)
    both_ref[...] = jnp.concatenate([x[:planes, :], z[:planes, :]], axis=0).astype(jnp.bfloat16)


def logits_kernel(
    edge, parts, total, devices, scale,
    orient_ref, allowed_ref, got_ref, own_ref, far_ref, out_ref,
    wide_f32, flat, turned, kinds, rotated, shifted,
):
    h = edge // parts
    planes = 2 * h
    wide = edge * edge
    columns = wide // LANES
    spare = ROWS - h - 2
    span = 4 * h * edge
    me = lax.axis_index("dp")
    for j in range(columns):
        wide_f32[j] = got_ref[:, j * LANES : (j + 1) * LANES].astype(jnp.float32)
    own = own_ref[...].astype(jnp.float32)
    far = far_ref[...].astype(jnp.float32)
    for turn in range(2):
        kinds[2 * turn, :planes, :] = own[turn * planes : (turn + 1) * planes, :]
        for c in range(2):
            for l in range(h):
                row = turn * planes + c * h + h - 1 - l
                kinds[2 * turn + 1, c * h + l : c * h + l + 1, :] = far[row : row + 1, :]
    for axis in (1, 2):
        for side in range(2):
            for c in range(2):
                for jl in range(h):
                    q, e = divmod(c * h + jl, spare)
                    for pair in range(h // 2):
                        left = q * span + (axis - 1) * 2 * h * edge + side * h * edge + pair * LANES
                        for s in range(0, parts, ROWS):
                            block = wide_f32[left // LANES, pl.ds(s * ROWS + h + 2 + e, ROWS, stride=ROWS), :]
                            for parity in range(2):
                                l = 2 * pair + parity
                                if side == 1:
                                    l = h - 1 - l
                                base = (c * h + l) * edge + s * h + jl
                                flat[pl.ds(base, ROWS, stride=h), :] = swap_halves(block) if parity else block
            transpose_planes(flat, turned, planes, edge)
            for turn, planar in enumerate((flat, turned)):
                kind = axis * 4 + turn * 2 + side

                def store(m, value, kind=kind):
                    kinds[kind, :planes, m * LANES : (m + 1) * LANES] = value

                flatten_planes(planar, planes, edge, store)
    lane = lane_iota((ROWS, LANES))
    for o in range(total):
        c = o // ORI
        axis, first, second = (orient_ref[o, k] for k in range(3))
        flips = [orient_ref[o, 3 + k] for k in range(3)]
        turn = (first > second).astype(jnp.int32)
        kind = axis * 4 + turn * 2 + flips[0]
        index = lane ^ (flips[1] * edge + flips[2] * (edge - 1))
        for j in range(columns):
            at = j + flips[1] * (columns - 1 - 2 * j)
            value = kinds[kind, :, pl.ds(pl.multiple_of(at * LANES, LANES), LANES)]
            value = jnp.take_along_axis(value, index, axis=1, mode="promise_in_bounds")
            rotated[o * h : (o + 1) * h, j * LANES : (j + 1) * LANES] = value[c * h : (c + 1) * h, :]
    rows = total * h
    lane = lane_iota((rows, LANES))
    low = lane < edge
    after = (lane // edge) * edge + (lane + 1) % edge
    before = (lane // edge) * edge + (lane + edge - 1) % edge

    def swapped(j):
        j = j % columns
        return swap_halves(rotated[:, j * LANES : (j + 1) * LANES])

    for j in range(columns):
        at = slice(j * LANES, (j + 1) * LANES)
        value = rotated[:, at]
        here = swapped(j)
        results = [
            value,
            jnp.where(low, swapped(j - 1), here),
            jnp.where(low, here, swapped(j + 1)),
            jnp.take_along_axis(value, before, axis=1, mode="promise_in_bounds"),
            jnp.take_along_axis(value, after, axis=1, mode="promise_in_bounds"),
        ]
        for number, result in enumerate(results):
            shifted[number * rows : (number + 1) * rows, at] = result.astype(jnp.bfloat16)
    gram = lax.dot_general(
        shifted[...], got_ref[...], (((1,), (1,)), ((), ())), preferred_element_type=jnp.float32
    )
    many = parts * ROWS
    plane = lax.broadcasted_iota(jnp.int32, (rows, many), 0) % h
    mate = lax.broadcasted_iota(jnp.int32, (rows, many), 1) % ROWS
    kept = []
    for t, move in enumerate(MOVES):
        source = FLAT.index((move[1], move[2]))
        block = gram[source * rows : (source + 1) * rows, :]
        kept.append(jnp.where(mate == plane + 1 + move[0], block, 0.0))
    kept = jnp.concatenate(kept, axis=1)
    tall = lax.broadcasted_iota(jnp.int32, (total, rows), 1) // h
    adder = (tall == lax.broadcasted_iota(jnp.int32, (total, rows), 0)).astype(jnp.float32)
    shape = (len(MOVES) * many, SLOTS * parts)
    source = lax.broadcasted_iota(jnp.int32, shape, 0) // ROWS
    picker = (source == lax.broadcasted_iota(jnp.int32, shape, 1)).astype(jnp.float32)
    exact = functools.partial(jnp.dot, preferred_element_type=jnp.float32, precision=lax.Precision.HIGHEST)
    result = exact(exact(adder, kept), picker) * scale
    where = lax.broadcasted_iota(jnp.int32, result.shape, 1)
    kin = lax.broadcasted_iota(jnp.int32, result.shape, 0) // ORI
    permit = jnp.zeros(result.shape, jnp.int32)
    for c in range(total // ORI):
        permit = jnp.where(kin == c, allowed_ref[0, c], permit)
    barred = (where % parts == me) & (permit == 0)
    result = result + jnp.where(barred, jnp.float32(BARRED), jnp.float32(0.0))
    for d in range(devices):
        out_ref[d * total : (d + 1) * total, :] = result


def sums_kernel(edge, parts, total, groups, *refs):
    parts_in = refs[1 : 1 + groups]
    logits_ref = refs[0]
    out_ref, log_ref, chances, table = refs[1 + groups :]
    h = edge // parts
    wide = edge * edge
    columns = wide // LANES
    owned = total // groups
    rows = owned * h
    many = parts * ROWS
    span = SLOTS * parts
    mine, me = lax.axis_index("ref"), lax.axis_index("dp")
    lane = lane_iota((total, span))
    log_evidence = jnp.zeros((1, span), jnp.float32)
    for g in range(groups):
        score = logits_ref[g * parts * total : (g * parts + 1) * total, :]
        for s in range(1, parts):
            top = (g * parts + s) * total
            score = score + logits_ref[top : top + total, :]
        score = jnp.where(lane >= len(MOVES) * parts, jnp.float32(-3e38), score)
        peak = jnp.max(score, axis=0, keepdims=True)
        for step in (1, 2, 4):
            peak = jnp.maximum(peak, pltpu.roll(peak, step * parts, 1))
        expo = jnp.exp(score - peak)
        mass = jnp.sum(expo, axis=0, keepdims=True)
        for step in (1, 2, 4):
            mass = mass + pltpu.roll(mass, step * parts, 1)
        chances[g] = (expo / mass).astype(jnp.bfloat16)
        log_evidence = jnp.where(mine == g, peak + jnp.log(mass), log_evidence)
    log_ref[...] = jnp.sum(jnp.where(lane_iota((1, span)) == me, log_evidence, 0.0), axis=1, keepdims=True)
    at = mine * owned + lax.broadcasted_iota(jnp.int32, (rows, total), 0) // h
    chooser = (at == lax.broadcasted_iota(jnp.int32, (rows, total), 1)).astype(jnp.bfloat16)
    shape = (span, len(MOVES) * many)
    target = lax.broadcasted_iota(jnp.int32, shape, 1) // ROWS
    spread = (target == lax.broadcasted_iota(jnp.int32, shape, 0)).astype(jnp.bfloat16)
    plane = lax.broadcasted_iota(jnp.int32, (rows, many), 0) % h
    mate = lax.broadcasted_iota(jnp.int32, (rows, many), 1) % ROWS
    dot = functools.partial(jnp.dot, preferred_element_type=jnp.float32)
    total_sums = None
    for k in range(groups):
        g = lax.rem(mine + groups - k, groups)
        chosen = dot(chooser, chances[g]).astype(jnp.bfloat16)
        laid = dot(chosen, spread)
        blocks = [jnp.zeros((rows, many), jnp.float32)] * len(FLAT)
        for t, move in enumerate(MOVES):
            slot = FLAT.index((move[1], move[2]))
            block = laid[:, t * many : (t + 1) * many]
            blocks[slot] = jnp.where(mate == plane + 1 + move[0], block, blocks[slot])
        weights = jnp.concatenate(blocks, axis=0).astype(jnp.bfloat16)
        part = dot(weights, parts_in[k][...])
        if k == 0:
            table[...] = part
        else:
            table[...] += part
    lane = lane_iota((rows, LANES))
    low = lane < edge
    after = (lane // edge) * edge + (lane + 1) % edge
    before = (lane // edge) * edge + (lane + edge - 1) % edge

    def cut(slot, j):
        j = j % columns
        return table[slot * rows : (slot + 1) * rows, j * LANES : (j + 1) * LANES]

    for j in range(columns):
        value = cut(0, j)
        value = value + jnp.where(low, swap_halves(cut(1, j)), swap_halves(cut(1, j + 1)))
        value = value + jnp.where(low, swap_halves(cut(2, j - 1)), swap_halves(cut(2, j)))
        value = value + jnp.take_along_axis(cut(3, j), after, axis=1, mode="promise_in_bounds")
        value = value + jnp.take_along_axis(cut(4, j), before, axis=1, mode="promise_in_bounds")
        for o in range(owned):
            out_ref[o, :, j * LANES : (j + 1) * LANES] = value[o * h : (o + 1) * h, :]


def in_vmem():
    return pl.BlockSpec(memory_space=pltpu.VMEM)


def in_smem():
    return pl.BlockSpec(memory_space=pltpu.SMEM)


def per_device(particles, references, orient, allowed):
    edge = particles.shape[1]
    wide = edge * edge
    total = orient.shape[0]
    parts = lax.axis_size("dp")
    groups = lax.axis_size("ref")
    devices = parts * groups
    h = edge // parts
    planes = 2 * h
    scale = 3.0 / math.sqrt(edge**3)
    params = pltpu.CompilerParams(vmem_limit_bytes=VMEM_BYTES)
    f32, bf16 = jnp.float32, jnp.bfloat16
    sent, both = pl.pallas_call(
        functools.partial(pack_kernel, edge, parts),
        out_shape=(
            jax.ShapeDtypeStruct((parts * ROWS, wide), bf16),
            jax.ShapeDtypeStruct((2 * planes, wide), bf16),
        ),
        in_specs=[in_vmem()] * 2,
        out_specs=(in_vmem(), in_vmem()),
        scratch_shapes=[
            pltpu.VMEM((edge + 2 * ROWS, wide), f32),
            pltpu.VMEM((parts * ROWS, wide), f32),
            pltpu.VMEM((ROWS, wide), f32),
            pltpu.VMEM((ROWS, wide), f32),
            pltpu.VMEM((planes * edge, LANES), f32),
            pltpu.VMEM((planes * edge, LANES), f32),
        ],
        compiler_params=params,
        name="pack",
    )(particles.reshape(edge, wide), references)
    far = lax.ppermute(both, "dp", [(i, parts - 1 - i) for i in range(parts)])
    got = lax.all_to_all(sent, "dp", 0, 0, tiled=True)
    others = [
        lax.ppermute(got, "ref", [(i, (i + k) % groups) for i in range(groups)]) for k in range(1, groups)
    ]
    rows = total * h
    partial = pl.pallas_call(
        functools.partial(logits_kernel, edge, parts, total, devices, scale),
        out_shape=jax.ShapeDtypeStruct((devices * total, SLOTS * parts), f32),
        in_specs=[in_smem(), in_smem(), in_vmem(), in_vmem(), in_vmem()],
        out_specs=in_vmem(),
        scratch_shapes=[
            pltpu.VMEM((wide // LANES, parts * ROWS, LANES), f32),
            pltpu.VMEM((planes * edge, LANES), f32),
            pltpu.VMEM((planes * edge, LANES), f32),
            pltpu.VMEM((12, ROWS, wide), f32),
            pltpu.VMEM((rows, wide), f32),
            pltpu.VMEM((len(FLAT) * rows, wide), bf16),
        ],
        compiler_params=params,
        name="logits",
    )(orient, allowed, got, both, far)
    logits = lax.all_to_all(partial, ("ref", "dp"), 0, 0, tiled=True)
    owned = total // groups
    sums, log_evidence = pl.pallas_call(
        functools.partial(sums_kernel, edge, parts, total, groups),
        out_shape=(
            jax.ShapeDtypeStruct((owned, h, wide), f32),
            jax.ShapeDtypeStruct((1, 1), f32),
        ),
        in_specs=[in_vmem()] * (1 + groups),
        out_specs=(in_vmem(), in_vmem()),
        scratch_shapes=[
            pltpu.VMEM((groups, total, SLOTS * parts), bf16),
            pltpu.VMEM((len(FLAT) * owned * h, wide), f32),
        ],
        compiler_params=params,
        name="sums",
    )(logits, got, *others)
    return (sums, log_evidence.reshape(1))


def solution(mesh):
    return jax.shard_map(
        per_device,
        mesh=mesh,
        in_specs=(P(("ref", "dp"), None, None), P(None, "dp", None), P(), P(("ref", "dp"), None)),
        out_specs=(P("ref", "dp", None), P(("ref", "dp"))),
        check_vma=False,
    )
```

```python
import functools
import math

import jax
import jax.numpy as jnp
from jax import lax
from jax.experimental import pallas as pl
from jax.experimental.pallas import tpu as pltpu
from jax.sharding import PartitionSpec as P

ORI = 8
LANES = 128
ROWS = 8
MOVES = [(0, 0, 0), (1, 0, 0), (-1, 0, 0), (0, 1, 0), (0, -1, 0), (0, 0, 1), (0, 0, -1)]
FLAT = [(0, 0), (1, 0), (-1, 0), (0, 1), (0, -1)]
SLOTS = 8
BARRED = -1e30
VMEM_BYTES = 48 * 1024 * 1024
MOST_VMEM = 62 * 1024 * 1024


def lane_iota(shape):
    return lax.broadcasted_iota(jnp.int32, shape, len(shape) - 1)


def swap_halves(x):
    return pltpu.roll(x, LANES // 2, 1)


def transpose_planes(source, target, planes, edge):
    for n in range(0, planes, 2):
        turned = source[n * edge : (n + 2) * edge, :].T[:edge, :]
        target[n * edge : (n + 1) * edge, :] = turned
        target[(n + 1) * edge : (n + 2) * edge, :] = swap_halves(turned)


def flatten_planes(source, planes, edge, store):
    low = lane_iota((planes, LANES)) < edge
    for m in range(edge // 2):
        even = source[pl.ds(2 * m, planes, stride=edge), :]
        odd = source[pl.ds(2 * m + 1, planes, stride=edge), :]
        store(m, jnp.where(low, even, swap_halves(odd)))


def turn_rows(edge, planes, x, z, flat, turned):
    for m in range(edge // 2):
        piece = x[:planes, m * LANES : (m + 1) * LANES]
        flat[pl.ds(2 * m, planes, stride=edge), :] = piece
        flat[pl.ds(2 * m + 1, planes, stride=edge), :] = swap_halves(piece)
    transpose_planes(flat, turned, planes, edge)

    def store(m, value):
        z[:planes, m * LANES : (m + 1) * LANES] = value

    flatten_planes(turned, planes, edge, store)


def pack_kernel(
    edge, parts, part_hbm, refs_hbm, out_ref, both_ref, part_ref, refs_ref, sems, ring, stage, x, z, flat, turned
):
    h = edge // parts
    planes = 2 * h
    wide = edge * edge
    spare = ROWS - h - 2
    span = 4 * h * edge
    refs_copy = pltpu.make_async_copy(refs_hbm, refs_ref, sems.at[0])
    part_copy = pltpu.make_async_copy(part_hbm, part_ref, sems.at[1])
    refs_copy.start()
    part_copy.start()
    refs_copy.wait()
    for c in range(2):
        x[c * h : (c + 1) * h, :] = refs_ref[c].astype(jnp.float32)
    turn_rows(edge, planes, x, z, flat, turned)
    part_copy.wait()
    ring[ROWS : ROWS + edge, :] = part_ref[...].astype(jnp.float32)
    ring[ROWS - 1 : ROWS, :] = ring[ROWS + edge - 1 : ROWS + edge, :]
    ring[ROWS + edge : ROWS + edge + 1, :] = ring[ROWS : ROWS + 1, :]
    if planes // spare * span < wide:
        stage[...] = jnp.zeros_like(stage)
    slab = h * edge
    for s in range(parts):
        top = s * ROWS
        stage[top : top + h + 2, :] = ring[ROWS + h * s - 1 : ROWS + h * s + h + 1, :]
        mirror = parts - 1 - s
        for q in range(planes // spare):
            rows = slice(q * spare, (q + 1) * spare)
            for number, (array, place) in enumerate(((x, s), (x, mirror), (z, s), (z, mirror))):
                left = q * span + number * slab
                stage[top + h + 2 : top + ROWS, left : left + slab] = array[rows, place * slab : (place + 1) * slab]
    out_ref[...] = stage[...].astype(jnp.bfloat16)
    both_ref[...] = jnp.concatenate([x[:planes, :], z[:planes, :]], axis=0).astype(jnp.bfloat16)


def near_kernel(h, edge, own_ref, far_ref, out_ref, x, z, flat, turned):
    planes = 2 * h
    own = own_ref[...].astype(jnp.float32)
    for c in range(2):
        far = far_ref[c].astype(jnp.float32)
        for l in range(h):
            x[c * h + l : c * h + l + 1, :] = far[h - 1 - l : h - l, :]
    turn_rows(edge, planes, x, z, flat, turned)
    for turn in range(2):
        out_ref[2 * turn, :planes, :] = own[turn * planes : (turn + 1) * planes, :]
    out_ref[1, :planes, :] = x[:planes, :]
    out_ref[3, :planes, :] = z[:planes, :]


def logits_kernel(
    edge, parts, total, devices, scale,
    orient_ref, allowed_ref, got_ref, near_ref, out_ref,
    wide_f32, flat, turned, kinds, rotated, shifted,
):
    h = edge // parts
    planes = 2 * h
    wide = edge * edge
    columns = wide // LANES
    spare = ROWS - h - 2
    span = 4 * h * edge
    me = lax.axis_index("dp")
    for j in range(columns):
        wide_f32[j] = got_ref[:, j * LANES : (j + 1) * LANES].astype(jnp.float32)
    kinds[:4] = near_ref[...]
    for axis in (1, 2):
        for side in range(2):
            for c in range(2):
                for jl in range(h):
                    q, e = divmod(c * h + jl, spare)
                    for pair in range(h // 2):
                        left = q * span + (axis - 1) * 2 * h * edge + side * h * edge + pair * LANES
                        for s in range(0, parts, ROWS):
                            block = wide_f32[left // LANES, pl.ds(s * ROWS + h + 2 + e, ROWS, stride=ROWS), :]
                            for parity in range(2):
                                l = 2 * pair + parity
                                if side == 1:
                                    l = h - 1 - l
                                base = (c * h + l) * edge + s * h + jl
                                flat[pl.ds(base, ROWS, stride=h), :] = swap_halves(block) if parity else block
            transpose_planes(flat, turned, planes, edge)
            for turn, planar in enumerate((flat, turned)):
                kind = axis * 4 + turn * 2 + side

                def store(m, value, kind=kind):
                    kinds[kind, :planes, m * LANES : (m + 1) * LANES] = value

                flatten_planes(planar, planes, edge, store)
    lane = lane_iota((ROWS, LANES))
    for o in range(total):
        c = o // ORI
        axis, first, second = (orient_ref[o, k] for k in range(3))
        flips = [orient_ref[o, 3 + k] for k in range(3)]
        turn = (first > second).astype(jnp.int32)
        kind = axis * 4 + turn * 2 + flips[0]
        index = lane ^ (flips[1] * edge + flips[2] * (edge - 1))
        for j in range(columns):
            at = j + flips[1] * (columns - 1 - 2 * j)
            value = kinds[kind, :, pl.ds(pl.multiple_of(at * LANES, LANES), LANES)]
            value = jnp.take_along_axis(value, index, axis=1, mode="promise_in_bounds")
            rotated[o * h : (o + 1) * h, j * LANES : (j + 1) * LANES] = value[c * h : (c + 1) * h, :]
    rows = total * h
    lane = lane_iota((rows, LANES))
    low = lane < edge
    after = (lane // edge) * edge + (lane + 1) % edge
    before = (lane // edge) * edge + (lane + edge - 1) % edge

    def swapped(j):
        j = j % columns
        return swap_halves(rotated[:, j * LANES : (j + 1) * LANES])

    for j in range(columns):
        at = slice(j * LANES, (j + 1) * LANES)
        value = rotated[:, at]
        here = swapped(j)
        results = [
            value,
            jnp.where(low, swapped(j - 1), here),
            jnp.where(low, here, swapped(j + 1)),
            jnp.take_along_axis(value, before, axis=1, mode="promise_in_bounds"),
            jnp.take_along_axis(value, after, axis=1, mode="promise_in_bounds"),
        ]
        for number, result in enumerate(results):
            shifted[number * rows : (number + 1) * rows, at] = result.astype(jnp.bfloat16)
    gram = lax.dot_general(
        shifted[...], got_ref[...], (((1,), (1,)), ((), ())), preferred_element_type=jnp.float32
    )
    many = parts * ROWS
    plane = lax.broadcasted_iota(jnp.int32, (rows, many), 0) % h
    mate = lax.broadcasted_iota(jnp.int32, (rows, many), 1) % ROWS
    kept = []
    for t, move in enumerate(MOVES):
        source = FLAT.index((move[1], move[2]))
        block = gram[source * rows : (source + 1) * rows, :]
        kept.append(jnp.where(mate == plane + 1 + move[0], block, 0.0))
    kept = jnp.concatenate(kept, axis=1)
    tall = lax.broadcasted_iota(jnp.int32, (total, rows), 1) // h
    adder = (tall == lax.broadcasted_iota(jnp.int32, (total, rows), 0)).astype(jnp.float32)
    shape = (len(MOVES) * many, SLOTS * parts)
    source = lax.broadcasted_iota(jnp.int32, shape, 0) // ROWS
    picker = (source == lax.broadcasted_iota(jnp.int32, shape, 1)).astype(jnp.float32)
    exact = functools.partial(jnp.dot, preferred_element_type=jnp.float32, precision=lax.Precision.HIGHEST)
    result = exact(exact(adder, kept), picker) * scale
    where = lax.broadcasted_iota(jnp.int32, result.shape, 1)
    kin = lax.broadcasted_iota(jnp.int32, result.shape, 0) // ORI
    permit = jnp.zeros(result.shape, jnp.int32)
    for c in range(total // ORI):
        permit = jnp.where(kin == c, allowed_ref[0, c], permit)
    barred = (where % parts == me) & (permit == 0)
    result = result + jnp.where(barred, jnp.float32(BARRED), jnp.float32(0.0))
    for d in range(devices):
        out_ref[d * total : (d + 1) * total, :] = result


def sums_kernel(edge, parts, total, groups, *refs):
    parts_in = refs[1 : 1 + groups]
    logits_ref = refs[0]
    out_ref, log_ref, chances, table = refs[1 + groups :]
    h = edge // parts
    wide = edge * edge
    columns = wide // LANES
    owned = total // groups
    rows = owned * h
    span = SLOTS * parts
    mine, me = lax.axis_index("ref"), lax.axis_index("dp")
    lane = lane_iota((total, span))
    log_evidence = jnp.zeros((1, span), jnp.float32)
    for g in range(groups):
        score = logits_ref[g * parts * total : (g * parts + 1) * total, :]
        for s in range(1, parts):
            top = (g * parts + s) * total
            score = score + logits_ref[top : top + total, :]
        score = jnp.where(lane >= len(MOVES) * parts, jnp.float32(-3e38), score)
        peak = jnp.max(score, axis=0, keepdims=True)
        for step in (1, 2, 4):
            peak = jnp.maximum(peak, pltpu.roll(peak, step * parts, 1))
        expo = jnp.exp(score - peak)
        mass = jnp.sum(expo, axis=0, keepdims=True)
        for step in (1, 2, 4):
            mass = mass + pltpu.roll(mass, step * parts, 1)
        chances[g] = (expo / mass).astype(jnp.bfloat16)
        log_evidence = jnp.where(mine == g, peak + jnp.log(mass), log_evidence)
    log_ref[...] = jnp.sum(jnp.where(lane_iota((1, span)) == me, log_evidence, 0.0), axis=1, keepdims=True)
    at = mine * owned + lax.broadcasted_iota(jnp.int32, (rows, total), 0) // h
    chooser = (at == lax.broadcasted_iota(jnp.int32, (rows, total), 1)).astype(jnp.bfloat16)

    def tables(each):
        many = parts * each
        shape = (span, len(MOVES) * many)
        target = lax.broadcasted_iota(jnp.int32, shape, 1) // each
        spread = (target == lax.broadcasted_iota(jnp.int32, shape, 0)).astype(jnp.bfloat16)
        plane = lax.broadcasted_iota(jnp.int32, (rows, many), 0) % h
        mate = lax.broadcasted_iota(jnp.int32, (rows, many), 1) % each
        return many, spread, mate - plane

    dot = functools.partial(jnp.dot, preferred_element_type=jnp.float32)
    for k in range(groups):
        g = lax.rem(mine + groups - k, groups)
        many, spread, offset = tables(ROWS if k == 0 else h + 2)
        chosen = dot(chooser, chances[g]).astype(jnp.bfloat16)
        laid = dot(chosen, spread)
        blocks = [jnp.zeros((rows, many), jnp.float32)] * len(FLAT)
        for t, move in enumerate(MOVES):
            slot = FLAT.index((move[1], move[2]))
            block = laid[:, t * many : (t + 1) * many]
            blocks[slot] = jnp.where(offset == 1 + move[0], block, blocks[slot])
        weights = jnp.concatenate(blocks, axis=0).astype(jnp.bfloat16)
        part = dot(weights, parts_in[k][...])
        if k == 0:
            table[...] = part
        else:
            table[...] += part
    lane = lane_iota((rows, LANES))
    low = lane < edge
    after = (lane // edge) * edge + (lane + 1) % edge
    before = (lane // edge) * edge + (lane + edge - 1) % edge

    def cut(slot, j):
        j = j % columns
        return table[slot * rows : (slot + 1) * rows, j * LANES : (j + 1) * LANES]

    for j in range(columns):
        value = cut(0, j)
        value = value + jnp.where(low, swap_halves(cut(1, j)), swap_halves(cut(1, j + 1)))
        value = value + jnp.where(low, swap_halves(cut(2, j - 1)), swap_halves(cut(2, j)))
        value = value + jnp.take_along_axis(cut(3, j), after, axis=1, mode="promise_in_bounds")
        value = value + jnp.take_along_axis(cut(4, j), before, axis=1, mode="promise_in_bounds")
        for o in range(owned):
            out_ref[o, :, j * LANES : (j + 1) * LANES] = value[o * h : (o + 1) * h, :]


def trim_kernel(h, got_ref, out_ref):
    count, wide = got_ref.shape[0] // ROWS, got_ref.shape[1]
    whole = got_ref[...].reshape(count, ROWS, wide)
    out_ref[...] = whole[:, : h + 2, :].reshape(count * (h + 2), wide)


def in_vmem():
    return pl.BlockSpec(memory_space=pltpu.VMEM)


def in_smem():
    return pl.BlockSpec(memory_space=pltpu.SMEM)


def per_device(particles, references, orient, allowed):
    edge = particles.shape[1]
    wide = edge * edge
    total = orient.shape[0]
    parts = lax.axis_size("dp")
    groups = lax.axis_size("ref")
    devices = parts * groups
    h = edge // parts
    planes = 2 * h
    scale = 3.0 / math.sqrt(edge**3)
    params = pltpu.CompilerParams(vmem_limit_bytes=VMEM_BYTES)
    f32, bf16 = jnp.float32, jnp.bfloat16
    far = lax.ppermute(references, "dp", [(i, parts - 1 - i) for i in range(parts)])
    sent, both = pl.pallas_call(
        functools.partial(pack_kernel, edge, parts),
        out_shape=(
            jax.ShapeDtypeStruct((parts * ROWS, wide), bf16),
            jax.ShapeDtypeStruct((2 * planes, wide), bf16),
        ),
        in_specs=[pl.BlockSpec(memory_space=pl.ANY)] * 2,
        out_specs=(in_vmem(), in_vmem()),
        scratch_shapes=[
            pltpu.VMEM((edge, wide), bf16),
            pltpu.VMEM(references.shape, bf16),
            pltpu.SemaphoreType.DMA((2,)),
            pltpu.VMEM((edge + 2 * ROWS, wide), f32),
            pltpu.VMEM((parts * ROWS, wide), f32),
            pltpu.VMEM((ROWS, wide), f32),
            pltpu.VMEM((ROWS, wide), f32),
            pltpu.VMEM((planes * edge, LANES), f32),
            pltpu.VMEM((planes * edge, LANES), f32),
        ],
        compiler_params=pltpu.CompilerParams(vmem_limit_bytes=MOST_VMEM),
        name="pack",
    )(particles.reshape(edge, wide), references)
    near = pl.pallas_call(
        functools.partial(near_kernel, h, edge),
        out_shape=jax.ShapeDtypeStruct((4, ROWS, wide), f32),
        in_specs=[in_vmem()] * 2,
        out_specs=in_vmem(),
        scratch_shapes=[
            pltpu.VMEM((ROWS, wide), f32),
            pltpu.VMEM((ROWS, wide), f32),
            pltpu.VMEM((planes * edge, LANES), f32),
            pltpu.VMEM((planes * edge, LANES), f32),
        ],
        compiler_params=params,
        cost_estimate=pl.CostEstimate(flops=0, bytes_accessed=16 * 1024 * 1024, transcendentals=0),
        name="near",
    )(both, far)
    got = lax.all_to_all(sent, "dp", 0, 0, tiled=True)
    got, near = lax.optimization_barrier((got, near))
    trimmed = pl.pallas_call(
        functools.partial(trim_kernel, h),
        out_shape=jax.ShapeDtypeStruct((parts * (h + 2), wide), bf16),
        in_specs=[in_vmem()],
        out_specs=in_vmem(),
        compiler_params=params,
        name="trim",
    )(got)
    others = [
        lax.ppermute(trimmed, "ref", [(i, (i + k) % groups) for i in range(groups)]) for k in range(1, groups)
    ]
    rows = total * h
    partial = pl.pallas_call(
        functools.partial(logits_kernel, edge, parts, total, devices, scale),
        out_shape=jax.ShapeDtypeStruct((devices * total, SLOTS * parts), f32),
        in_specs=[in_smem(), in_smem(), in_vmem(), in_vmem()],
        out_specs=in_vmem(),
        scratch_shapes=[
            pltpu.VMEM((wide // LANES, parts * ROWS, LANES), f32),
            pltpu.VMEM((planes * edge, LANES), f32),
            pltpu.VMEM((planes * edge, LANES), f32),
            pltpu.VMEM((12, ROWS, wide), f32),
            pltpu.VMEM((rows, wide), f32),
            pltpu.VMEM((len(FLAT) * rows, wide), bf16),
        ],
        compiler_params=params,
        name="logits",
    )(orient, allowed, got, near)
    logits = lax.all_to_all(partial, ("ref", "dp"), 0, 0, tiled=True)
    owned = total // groups
    sums, log_evidence = pl.pallas_call(
        functools.partial(sums_kernel, edge, parts, total, groups),
        out_shape=(
            jax.ShapeDtypeStruct((owned, h, wide), f32),
            jax.ShapeDtypeStruct((1, 1), f32),
        ),
        in_specs=[in_vmem()] * (1 + groups),
        out_specs=(in_vmem(), in_vmem()),
        scratch_shapes=[
            pltpu.VMEM((groups, total, SLOTS * parts), bf16),
            pltpu.VMEM((len(FLAT) * owned * h, wide), f32),
        ],
        compiler_params=params,
        name="sums",
    )(logits, got, *others)
    return (sums, log_evidence.reshape(1))


def solution(mesh):
    return jax.shard_map(
        per_device,
        mesh=mesh,
        in_specs=(P(("ref", "dp"), None, None), P(None, "dp", None), P(), P(("ref", "dp"), None)),
        out_specs=(P("ref", "dp", None), P(("ref", "dp"))),
        check_vma=False,
    )
```

```python
import functools
import math

import jax
import jax.numpy as jnp
from jax import lax
from jax.experimental import pallas as pl
from jax.experimental.pallas import tpu as pltpu
from jax.sharding import PartitionSpec as P

ORI = 8
LANES = 128
ROWS = 8
MOVES = [(0, 0, 0), (1, 0, 0), (-1, 0, 0), (0, 1, 0), (0, -1, 0), (0, 0, 1), (0, 0, -1)]
FLAT = [(0, 0), (1, 0), (-1, 0), (0, 1), (0, -1)]
SLOTS = 8
BARRED = -1e30
VMEM_BYTES = 24 * 1024 * 1024
MOST_VMEM = 62 * 1024 * 1024


def lane_iota(shape):
    return lax.broadcasted_iota(jnp.int32, shape, len(shape) - 1)


def row_iota(shape):
    return lax.broadcasted_iota(jnp.int32, shape, 0)


def swap_halves(x):
    return pltpu.roll(x, LANES // 2, 1)


def pick_lanes(x, index):
    return jnp.take_along_axis(x, index, axis=1, mode="promise_in_bounds")


def tile(m):
    return slice(m * LANES, (m + 1) * LANES)


def outer_inner(h, me):
    outer = (me % 2) * (h + 1)
    return outer, h + 1 - outer


def turn_rows(edge, planes, x, z, flat, turned):
    low = lane_iota((planes, LANES)) < edge
    for m in range(edge // 2):
        piece = x[:planes, tile(m)]
        flat[pl.ds(2 * m, planes, stride=edge), :] = piece
        flat[pl.ds(2 * m + 1, planes, stride=edge), :] = swap_halves(piece)
    for n in range(0, planes, 2):
        block = flat[n * edge : (n + 2) * edge, :].T[:edge, :]
        turned[n * edge : (n + 1) * edge, :] = block
        turned[(n + 1) * edge : (n + 2) * edge, :] = swap_halves(block)
    for m in range(edge // 2):
        even = turned[pl.ds(2 * m, planes, stride=edge), :]
        odd = turned[pl.ds(2 * m + 1, planes, stride=edge), :]
        z[:planes, tile(m)] = jnp.where(low, even, swap_halves(odd))


def pack_kernel(
    edge, parts, part_hbm, refs_hbm, out_ref, both_ref, part_ref, refs_ref, sems, ring, stage, x, z, flat, turned
):
    h = edge // parts
    planes = 2 * h
    wide = edge * edge
    spare = ROWS - h - 2
    span = 4 * h * edge
    chunk = 2 * ROWS
    refs_copy = pltpu.make_async_copy(refs_hbm, refs_ref, sems.at[0])
    refs_copy.start()
    copies = []
    for i in range(edge // chunk):
        rows = pl.ds(i * chunk, chunk)
        copies.append(pltpu.make_async_copy(part_hbm.at[rows], part_ref.at[rows], sems.at[1 + i]))
        copies[-1].start()
    refs_copy.wait()
    for c in range(2):
        x[c * h : (c + 1) * h, :] = refs_ref[c].astype(jnp.float32)
    turn_rows(edge, planes, x, z, flat, turned)
    both_ref[...] = jnp.concatenate([x[:planes, :], z[:planes, :]], axis=0).astype(jnp.bfloat16)
    if planes // spare * span < wide:
        stage[...] = jnp.zeros_like(stage)
    slab = h * edge
    for s in range(parts):
        top = s * ROWS
        mirror = parts - 1 - s
        for q in range(planes // spare):
            rows = slice(q * spare, (q + 1) * spare)
            for number, (array, place) in enumerate(((x, s), (x, mirror), (z, s), (z, mirror))):
                left = q * span + number * slab
                stage[top + h + 2 : top + ROWS, left : left + slab] = array[rows, place * slab : (place + 1) * slab]
    last = len(copies) - 1
    done = 0
    for i in [last] + list(range(last)):
        copies[i].wait()
        rows = slice(i * chunk, (i + 1) * chunk)
        ring[ROWS + i * chunk : ROWS + (i + 1) * chunk, :] = part_ref[rows, :].astype(jnp.float32)
        if i == last:
            ring[ROWS - 1 : ROWS, :] = ring[ROWS + edge - 1 : ROWS + edge, :]
        if i == 0:
            ring[ROWS + edge : ROWS + edge + 1, :] = ring[ROWS : ROWS + 1, :]
        ready = 0 if i == last else (parts if i == last - 1 else ((i + 1) * chunk - 1) // h)
        while done + 2 <= ready:
            for s in (done, done + 1):
                top, first = s * ROWS, ROWS + h * s
                stage[top : top + h, :] = ring[first : first + h, :]
                ends = (first - 1, first + h) if s % 2 == 0 else (first + h, first - 1)
                for number, end in enumerate(ends):
                    stage[top + h + number : top + h + number + 1, :] = ring[end : end + 1, :]
            both = slice(done * ROWS, (done + 2) * ROWS)
            out_ref[both, :] = stage[both, :].astype(jnp.bfloat16)
            done += 2


def near_kernel(edge, h, own_ref, far_ref, out_ref, x, z, flat, turned):
    planes = 2 * h
    columns = edge * edge // LANES
    own = own_ref[...].astype(jnp.float32)
    for c in range(2):
        far = far_ref[c].astype(jnp.float32)
        for l in range(h):
            x[c * h + l : c * h + l + 1, :] = far[h - 1 - l : h - l, :]
    turn_rows(edge, planes, x, z, flat, turned)
    for turn in range(2):
        far = (x, z)[turn]
        for c in range(2):
            for copy in range(ROWS // h):
                rows = slice(copy * h, (copy + 1) * h)
                top = turn * planes + c * h
                for m in range(columns):
                    out_ref[(turn * 4 + c) * columns + m, rows, :] = own[top : top + h, tile(m)]
                    out_ref[(turn * 4 + 2 + c) * columns + m, rows, :] = far[c * h : (c + 1) * h, tile(m)]


def logits_kernel(
    edge, parts, total, devices, scale,
    orient_ref, allowed_ref, got_ref, near_ref, out_ref,
    wide_f32, flat, turned, kinds, shifted, gram,
):
    h = edge // parts
    planes = 2 * h
    wide = edge * edge
    columns = wide // LANES
    spare = ROWS - h - 2
    span = 4 * h * edge
    rows = total * h
    me = lax.axis_index("dp")
    low = lane_iota((ROWS, LANES)) < edge
    for j in range(columns):
        wide_f32[j] = got_ref[:, tile(j)].astype(jnp.float32)
    kinds[: 8 * columns] = near_ref[...]

    def keep(first, second, value, m):
        if planes == ROWS:
            upper = row_iota((ROWS, LANES)) < h
            other = pltpu.roll(value, h, 0)
            kinds[first * columns + m] = jnp.where(upper, value, other)
            kinds[second * columns + m] = jnp.where(upper, other, value)
        else:
            for number, kind in enumerate((first, second)):
                for copy in range(ROWS // h):
                    kinds[kind * columns + m, copy * h : (copy + 1) * h, :] = value[number * h : (number + 1) * h, :]

    for axis in (1, 2):
        for c in range(2):
            for jl in range(h):
                q, e = divmod(c * h + jl, spare)
                first = (q * span + (axis - 1) * 2 * h * edge) // LANES
                for s in range(0, parts, ROWS):
                    tiles = [
                        wide_f32[first + i, pl.ds(s * ROWS + h + 2 + e, ROWS, stride=ROWS), :] for i in range(h)
                    ]
                    for l in range(h):
                        plain, mirrored = tiles[l // 2], tiles[h // 2 + (h - 1 - l) // 2]
                        if l % 2 == 0:
                            value = jnp.where(low, plain, mirrored)
                        else:
                            value = swap_halves(jnp.where(low, mirrored, plain))
                        flat[pl.ds((c * h + l) * edge + s * h + jl, ROWS, stride=h), :] = value
        for l in range(h):
            block = jnp.concatenate(
                [flat[(c * h + l) * edge : (c * h + l + 1) * edge, :] for c in range(2)], axis=0
            ).T
            for side in range(2):
                turned[(side * h + l) * edge : (side * h + l + 1) * edge, :] = block[side * edge : (side + 1) * edge, :]
        part = lane_iota((planes, LANES)) < edge
        for m in range(edge // 2):
            even = flat[pl.ds(2 * m, planes, stride=edge), :]
            odd = flat[pl.ds(2 * m + 1, planes, stride=edge), :]
            keep(axis * 8, axis * 8 + 1, jnp.where(part, even, swap_halves(odd)), m)
            keep(axis * 8 + 2, axis * 8 + 3, jnp.where(part, swap_halves(even), odd), m)
            even = turned[pl.ds(2 * m, planes, stride=edge), :]
            odd = turned[pl.ds(2 * m + 1, planes, stride=edge), :]
            keep(axis * 8 + 4, axis * 8 + 6, jnp.where(part, even, swap_halves(odd)), m)
            keep(axis * 8 + 5, axis * 8 + 7, jnp.where(part, swap_halves(even), odd), m)

    lane = lane_iota((ROWS, LANES))
    slot = row_iota((ROWS, LANES)) // h
    per = ROWS // h
    lows = lane < edge
    after = (lane // edge) * edge + (lane + 1) % edge
    before = (lane // edge) * edge + (lane + edge - 1) % edge
    start, step, index = [], [], []
    for b in range(total // per):
        xor = jnp.zeros((ROWS, LANES), jnp.int32)
        for i in range(per):
            o = b * per + i
            turn = (orient_ref[o, 1] > orient_ref[o, 2]).astype(jnp.int32)
            kind = orient_ref[o, 0] * 8 + turn * 4 + orient_ref[o, 3] * 2 + o // ORI
            start.append(kind * columns + orient_ref[o, 4] * (columns - 1))
            step.append(1 - 2 * orient_ref[o, 4])
            xor = jnp.where(slot == i, orient_ref[o, 4] * edge + orient_ref[o, 5] * (edge - 1), xor)
        index.append([lane ^ xor, (lane ^ edge) ^ xor, before ^ xor, after ^ xor])

    def column(j):
        found = []
        for b in range(total // per):
            value = kinds[start[b * per] + j * step[b * per]]
            for i in range(1, per):
                value = jnp.where(slot == i, kinds[start[b * per + i] + j * step[b * per + i]], value)
            found.append([pick_lanes(value, way) for way in index[b]])
        return [list(way) for way in zip(*found, strict=True)]

    behind = column(columns - 1)[1]
    here = column(0)
    for j in range(columns):
        ahead = column((j + 1) % columns)
        results = [
            here[0],
            [jnp.where(lows, x, y) for x, y in zip(behind, here[1], strict=True)],
            [jnp.where(lows, x, y) for x, y in zip(here[1], ahead[1], strict=True)],
            here[2],
            here[3],
        ]
        for number, result in enumerate(results):
            shifted[number * rows : (number + 1) * rows, tile(j)] = jnp.concatenate(result, axis=0).astype(jnp.bfloat16)
        behind, here = here[1], ahead
    gram[...] = lax.dot_general(
        shifted[...], got_ref[...], (((1,), (1,)), ((), ())), preferred_element_type=jnp.float32
    )
    many = parts * ROWS
    place = lane_iota((total, many)) % ROWS
    outer, inner = outer_inner(h, me)
    mate = jnp.where(place < h, place + 1, jnp.where(place == h, outer, jnp.where(place == h + 1, inner, -h)))
    kept = []
    for t, move in enumerate(MOVES):
        source = FLAT.index((move[1], move[2]))
        total_t = None
        for l in range(h):
            if many == LANES:
                block = gram[pl.ds(source * rows + l, total, stride=h), :]
            else:
                block = jnp.concatenate(
                    [gram[source * rows + o * h + l : source * rows + o * h + l + 1, :] for o in range(total)], axis=0
                )
            block = jnp.where(mate == l + 1 + move[0], block, 0.0)
            total_t = block if total_t is None else total_t + block
        kept.append(total_t)
    if many == LANES:
        lane = lane_iota((total, LANES))
        result = jnp.zeros((total, LANES), jnp.float32)
        for t in range(len(MOVES)):
            value = kept[t]
            for step in (1, 2, 4):
                value = value + pltpu.roll(value, LANES - step, 1)
            result = jnp.where(lane // parts == t, pick_lanes(value, (lane % parts) * ROWS), result)
    else:
        shape = (len(MOVES) * many, SLOTS * parts)
        picker = (row_iota(shape) // ROWS == lane_iota(shape)).astype(jnp.float32)
        result = jnp.dot(
            jnp.concatenate(kept, axis=1), picker,
            preferred_element_type=jnp.float32, precision=lax.Precision.HIGHEST,
        )
    result = result * scale
    kin = row_iota(result.shape) // ORI
    permit = jnp.zeros(result.shape, jnp.int32)
    for c in range(total // ORI):
        permit = jnp.where(kin == c, allowed_ref[0, c], permit)
    barred = (lane_iota(result.shape) % parts == me) & (permit != 1)
    result = result + jnp.where(barred, jnp.float32(BARRED), jnp.float32(0.0))
    for d in range(devices):
        out_ref[d * total : (d + 1) * total, :] = result


def trim_kernel(h, got_ref, core_ref, outer_ref):
    count, wide = got_ref.shape[0] // ROWS, got_ref.shape[1]
    whole = got_ref[...].reshape(count, ROWS, wide)
    core_ref[...] = whole[:, :h, :].reshape(count * h, wide)
    outer_ref[...] = whole[:, h, :]


def edge_kernel(h, core_ref, out_ref, *tables):
    parts = core_ref.shape[0] // h
    whole = core_ref[...].reshape(parts, h, core_ref.shape[1])
    even = lax.axis_index("dp") % 2 == 0

    @pl.when(even)
    def _():
        out_ref[...] = whole[:, h - 1, :]

    @pl.when(jnp.logical_not(even))
    def _():
        out_ref[...] = whole[:, 0, :]

    for table, own in zip(tables, (True, False)):
        table[...] = spread_table(h, parts, own)


def far_columns(h, parts):
    return -(-parts * (h + 2) // LANES) * LANES


def spread_table(h, parts, own):
    many = parts * ROWS if own else far_columns(h, parts)
    shape = (SLOTS * parts, len(MOVES) * many)
    column = lane_iota(shape) % many
    if own:
        particle = column // ROWS
    else:
        particle = jnp.where(column < parts * h, column // h, column % parts)
    return ((lane_iota(shape) // many) * parts + particle == row_iota(shape)).astype(jnp.bfloat16)


def mate_row(h, parts, own, me):
    outer, inner = outer_inner(h, me)
    if own:
        place = lane_iota((ROWS, parts * ROWS)) % ROWS
        return jnp.where(place < h, place + 1, jnp.where(place == h, outer, jnp.where(place == h + 1, inner, -h)))
    column = lane_iota((ROWS, far_columns(h, parts)))
    mate = jnp.where(column < parts * h, column % h + 1, jnp.where(column < parts * (h + 1), outer, inner))
    return jnp.where(column < parts * (h + 2), mate, -h)


def sums_kernel(edge, parts, total, groups, logits_ref, own_table, far_table, got_ref, *refs):
    pieces, refs = refs[: 3 * (groups - 1)], refs[3 * (groups - 1) :]
    out_hbm, log_ref, out_ref, sems, in_sems, chances, weights, table, merged = refs
    h = edge // parts
    wide = edge * edge
    columns = wide // LANES
    owned = total // groups
    rows = owned * h
    span = SLOTS * parts
    mine, me = lax.axis_index("ref"), lax.axis_index("dp")
    incoming = []
    for number, piece in enumerate(pieces):
        if number % 3 == 0:
            top = got_ref.shape[0] + number // 3 * far_columns(h, parts)
        rows_here = pl.ds(top, piece.shape[0])
        incoming.append(pltpu.make_async_copy(piece, merged.at[rows_here], in_sems.at[number]))
        top += piece.shape[0]
        rest = far_columns(h, parts) - parts * (h + 2)
        if number % 3 == 2 and rest:
            merged[top : top + rest, :] = jnp.zeros((rest, wide), merged.dtype)
    for copy in incoming:
        copy.start()
    merged[: got_ref.shape[0], :] = got_ref[...]
    dot = functools.partial(jnp.dot, preferred_element_type=jnp.float32)
    lane = lane_iota((total, span))
    log_evidence = jnp.zeros((1, span), jnp.float32)
    for g in range(groups):
        scores = [logits_ref[(g * parts + s) * total : (g * parts + s + 1) * total, :] for s in range(parts)]
        while len(scores) > 1:
            scores = [sum(scores[i : i + 2]) for i in range(0, len(scores), 2)]
        score = jnp.where(lane >= len(MOVES) * parts, jnp.float32(-3e38), scores[0])
        peak = jnp.max(score, axis=0, keepdims=True)
        for step in (1, 2, 4):
            peak = jnp.maximum(peak, pltpu.roll(peak, step * parts, 1))
        expo = jnp.exp(score - peak)
        mass = jnp.sum(expo, axis=0, keepdims=True)
        for step in (1, 2, 4):
            mass = mass + pltpu.roll(mass, step * parts, 1)
        chances[g] = expo / mass
        log_evidence = jnp.where(mine == g, peak + jnp.log(mass), log_evidence)
    log_ref[...] = jnp.sum(jnp.where(lane_iota((1, span)) == me, log_evidence, 0.0), axis=1, keepdims=True)
    left = 0
    for k in range(groups):
        g = lax.rem(mine + groups - k, groups)
        if owned % ROWS == 0:
            chosen = chances[g, pl.ds(pl.multiple_of(mine * owned, ROWS), owned), :].astype(jnp.bfloat16)
        else:
            at = mine * owned + row_iota((owned, total))
            chooser = (at == lane_iota((owned, total))).astype(jnp.bfloat16)
            chosen = dot(chooser, chances[g].astype(jnp.bfloat16)).astype(jnp.bfloat16)
        laid = dot(chosen, (own_table if k == 0 else far_table)[...])
        mate = mate_row(h, parts, k == 0, me)[:owned]
        many = mate.shape[1]
        for slot in range(len(FLAT)):
            for l in range(h):
                value = jnp.zeros((owned, many), jnp.float32)
                for t, move in enumerate(MOVES):
                    if FLAT.index((move[1], move[2])) == slot:
                        value = jnp.where(mate == l + 1 + move[0], laid[:, t * many : (t + 1) * many], value)
                for m in range(many // LANES):
                    weights[left // LANES + m, pl.ds(slot * rows + l, owned, stride=h), :] = value[:, tile(m)]
        left += many
    both = jnp.concatenate([weights[m] for m in range(left // LANES)], axis=1).astype(jnp.bfloat16)
    for copy in incoming:
        copy.wait()
    table[...] = dot(both, merged[...])
    lane = lane_iota((rows, LANES))
    low = lane < edge
    after = (lane // edge) * edge + (lane + 1) % edge
    before = (lane // edge) * edge + (lane + edge - 1) % edge

    def cut(slot, j):
        return table[slot * rows : (slot + 1) * rows, tile(j % columns)]

    pieces = sems.shape[0]
    copies = []
    up = swap_halves(cut(1, 0))
    down = swap_halves(cut(2, columns - 1))
    for j in range(columns):
        up_next, down_next = swap_halves(cut(1, j + 1)), swap_halves(cut(2, j))
        value = cut(0, j) + jnp.where(low, up, up_next) + jnp.where(low, down, down_next)
        value = value + pick_lanes(cut(3, j), after) + pick_lanes(cut(4, j), before)
        up, down = up_next, down_next
        for o in range(owned):
            out_ref[o, :, tile(j)] = value[o * h : (o + 1) * h, :]
        if (j + 1) % (columns // pieces) == 0:
            number = len(copies)
            part = pl.ds(number * (wide // pieces), wide // pieces)
            copies.append(
                pltpu.make_async_copy(out_ref.at[:, :, part], out_hbm.at[:, :, part], sems.at[number])
            )
            copies[-1].start()
    for copy in copies:
        copy.wait()


def in_vmem():
    return pl.BlockSpec(memory_space=pltpu.VMEM)


def in_smem():
    return pl.BlockSpec(memory_space=pltpu.SMEM)


def anywhere():
    return pl.BlockSpec(memory_space=pl.ANY)


def per_device(particles, references, orient, allowed):
    edge = particles.shape[1]
    wide = edge * edge
    total = orient.shape[0]
    parts = lax.axis_size("dp")
    groups = lax.axis_size("ref")
    devices = parts * groups
    h = edge // parts
    planes = 2 * h
    rows = total * h
    owned = total // groups
    scale = 3.0 / math.sqrt(edge**3)
    params = pltpu.CompilerParams(vmem_limit_bytes=VMEM_BYTES)
    f32, bf16 = jnp.float32, jnp.bfloat16
    array = jax.ShapeDtypeStruct
    turning = [
        pltpu.VMEM((ROWS, wide), f32),
        pltpu.VMEM((ROWS, wide), f32),
        pltpu.VMEM((planes * edge, LANES), f32),
        pltpu.VMEM((planes * edge, LANES), f32),
    ]
    far = lax.ppermute(references, "dp", [(i, parts - 1 - i) for i in range(parts)])
    sent, both = pl.pallas_call(
        functools.partial(pack_kernel, edge, parts),
        out_shape=(array((parts * ROWS, wide), bf16), array((2 * planes, wide), bf16)),
        in_specs=[anywhere()] * 2,
        out_specs=(in_vmem(), in_vmem()),
        scratch_shapes=[
            pltpu.VMEM((edge, wide), bf16),
            pltpu.VMEM(references.shape, bf16),
            pltpu.SemaphoreType.DMA((1 + edge // (2 * ROWS),)),
            pltpu.VMEM((edge + 2 * ROWS, wide), f32),
            pltpu.VMEM((parts * ROWS, wide), f32),
            *turning,
        ],
        compiler_params=pltpu.CompilerParams(vmem_limit_bytes=MOST_VMEM),
        name="pack",
    )(particles.reshape(edge, wide), references)
    near = pl.pallas_call(
        functools.partial(near_kernel, edge, h),
        out_shape=array((8 * wide // LANES, ROWS, LANES), f32),
        in_specs=[in_vmem()] * 2,
        out_specs=in_vmem(),
        scratch_shapes=turning,
        compiler_params=params,
        cost_estimate=pl.CostEstimate(flops=0, bytes_accessed=16 * 1024 * 1024, transcendentals=0),
        name="near",
    )(both, far)
    got = lax.all_to_all(sent, "dp", 0, 0, tiled=True)
    got, near = lax.optimization_barrier((got, near))
    core, outer = pl.pallas_call(
        functools.partial(trim_kernel, h),
        out_shape=(array((parts * h, wide), bf16), array((parts, wide), bf16)),
        in_specs=[in_vmem()],
        out_specs=(in_vmem(), in_vmem()),
        compiler_params=params,
        name="trim",
    )(got)
    steps = [[(i, (i + k) % groups) for i in range(groups)] for k in range(1, groups)]
    cores = [lax.ppermute(core, "ref", step) for step in steps]
    partial = pl.pallas_call(
        functools.partial(logits_kernel, edge, parts, total, devices, scale),
        out_shape=array((devices * total, SLOTS * parts), f32),
        in_specs=[in_smem(), in_smem(), in_vmem(), in_vmem()],
        out_specs=in_vmem(),
        scratch_shapes=[
            pltpu.VMEM((wide // LANES, parts * ROWS, LANES), f32),
            pltpu.VMEM((planes * edge, LANES), f32),
            pltpu.VMEM((planes * edge, LANES), f32),
            pltpu.VMEM((24 * wide // LANES, ROWS, LANES), f32),
            pltpu.VMEM((len(FLAT) * rows, wide), bf16),
            pltpu.VMEM((len(FLAT) * rows, parts * ROWS), f32),
        ],
        compiler_params=params,
        name="logits",
    )(orient, allowed, got, near)
    partial, outer = lax.optimization_barrier((partial, outer))
    logits = lax.all_to_all(partial, ("ref", "dp"), 0, 0, tiled=True)
    span = SLOTS * parts
    tables = [array((span, len(MOVES) * n), bf16) for n in (parts * ROWS, far_columns(h, parts))]
    pieces = []
    for core, step in zip(cores, steps, strict=True):
        lacking, *laid = pl.pallas_call(
            functools.partial(edge_kernel, h),
            out_shape=(array((parts, wide), bf16), *tables),
            in_specs=[in_vmem()],
            out_specs=(in_vmem(),) * (1 + len(tables)),
            compiler_params=params,
            cost_estimate=pl.CostEstimate(flops=0, bytes_accessed=16 * 1024 * 1024, transcendentals=0),
            name="edges",
        )(core)
        if not pieces:
            spreads = laid
        pieces += [
            core,
            lax.ppermute(outer, "ref", step),
            lax.ppermute(lacking, "dp", [(i, i ^ 1) for i in range(parts)]),
        ]
        tables = []
    merged_rows = got.shape[0] + (groups - 1) * far_columns(h, parts)
    sums, log_evidence = pl.pallas_call(
        functools.partial(sums_kernel, edge, parts, total, groups),
        out_shape=(array((owned, h, wide), f32), array((1, 1), f32)),
        in_specs=[in_vmem()] * 4 + [anywhere()] * len(pieces),
        out_specs=(anywhere(), in_vmem()),
        scratch_shapes=[
            pltpu.VMEM((owned, h, wide), f32),
            pltpu.SemaphoreType.DMA((4,)),
            pltpu.SemaphoreType.DMA((len(pieces),)),
            pltpu.VMEM((groups, total, span), f32),
            pltpu.VMEM((merged_rows // LANES, len(FLAT) * owned * h, LANES), f32),
            pltpu.VMEM((len(FLAT) * owned * h, wide), f32),
            pltpu.VMEM((merged_rows, wide), bf16),
        ],
        compiler_params=params,
        name="sums",
    )(logits, *spreads, got, *pieces)
    return (sums, log_evidence.reshape(1))


def solution(mesh):
    return jax.shard_map(
        per_device,
        mesh=mesh,
        in_specs=(P(("ref", "dp"), None, None), P(None, "dp", None), P(), P(("ref", "dp"), None)),
        out_specs=(P("ref", "dp", None), P(("ref", "dp"))),
        check_vma=False,
    )
```

```python
import functools
import math

import jax
import jax.numpy as jnp
from jax import lax
from jax.experimental import pallas as pl
from jax.experimental.pallas import tpu as pltpu
from jax.sharding import PartitionSpec as P

ORI = 8
LANES = 128
ROWS = 8
MOVES = [(0, 0, 0), (1, 0, 0), (-1, 0, 0), (0, 1, 0), (0, -1, 0), (0, 0, 1), (0, 0, -1)]
FLAT = [(0, 0), (1, 0), (-1, 0), (0, 1), (0, -1)]
SLOTS = 8
BARRED = -1e30
VMEM_BYTES = 24 * 1024 * 1024
MOST_VMEM = 62 * 1024 * 1024


def lane_iota(shape):
    return lax.broadcasted_iota(jnp.int32, shape, len(shape) - 1)


def row_iota(shape):
    return lax.broadcasted_iota(jnp.int32, shape, 0)


def swap_halves(x):
    return pltpu.roll(x, LANES // 2, 1)


def rows_by_rows(a, b):
    return lax.dot_general(a, b, (((1,), (1,)), ((), ())), preferred_element_type=jnp.float32)


def pick_lanes(x, index):
    return jnp.take_along_axis(x, index, axis=1, mode="promise_in_bounds")


def tile(m):
    return slice(m * LANES, (m + 1) * LANES)


def lanes_of(edge, parts):
    h = edge // parts
    return edge * edge * h // ROWS, edge * edge // ROWS, 4 * h * edge


def turn_rows(edge, planes, x, z, flat, turned):
    low = lane_iota((planes, LANES)) < edge
    for m in range(edge // 2):
        piece = x[:planes, tile(m)]
        flat[pl.ds(2 * m, planes, stride=edge), :] = piece
        flat[pl.ds(2 * m + 1, planes, stride=edge), :] = swap_halves(piece)
    for n in range(0, planes, 2):
        block = flat[n * edge : (n + 2) * edge, :].T[:edge, :]
        turned[n * edge : (n + 1) * edge, :] = block
        turned[(n + 1) * edge : (n + 2) * edge, :] = swap_halves(block)
    for m in range(edge // 2):
        even = turned[pl.ds(2 * m, planes, stride=edge), :]
        odd = turned[pl.ds(2 * m + 1, planes, stride=edge), :]
        z[:planes, tile(m)] = jnp.where(low, even, swap_halves(odd))


def pack_kernel(
    edge, parts, part_hbm, refs_hbm, out_ref, both_ref, part_ref, refs_ref, sems, ring, stage, x, z, flat, turned
):
    h = edge // parts
    planes = 2 * h
    core, outer, _ = lanes_of(edge, parts)
    chunk = 2 * ROWS
    refs_copy = pltpu.make_async_copy(refs_hbm, refs_ref, sems.at[0])
    refs_copy.start()
    copies = []
    for i in range(edge // chunk):
        rows = pl.ds(i * chunk, chunk)
        copies.append(pltpu.make_async_copy(part_hbm.at[rows], part_ref.at[rows], sems.at[1 + i]))
        copies[-1].start()
    refs_copy.wait()
    for c in range(2):
        x[c * h : (c + 1) * h, :] = refs_ref[c].astype(jnp.float32)
    turn_rows(edge, planes, x, z, flat, turned)
    both_ref[...] = jnp.concatenate([x[:planes, :], z[:planes, :]], axis=0).astype(jnp.bfloat16)
    if planes < ROWS:
        stage[...] = jnp.zeros_like(stage)
    slab = h * edge
    for s in range(parts):
        top = s * ROWS
        mirror = parts - 1 - s
        for number, (array, place) in enumerate(((x, s), (x, mirror), (z, s), (z, mirror))):
            left = core + outer + number * slab
            stage[top : top + planes, left : left + slab] = array[:planes, place * slab : (place + 1) * slab]
    last = len(copies) - 1
    done = 0
    for i in [last] + list(range(last)):
        copies[i].wait()
        rows = slice(i * chunk, (i + 1) * chunk)
        ring[ROWS + i * chunk : ROWS + (i + 1) * chunk, :] = part_ref[rows, :].astype(jnp.float32)
        if i == last:
            ring[ROWS - 1 : ROWS, :] = ring[ROWS + edge - 1 : ROWS + edge, :]
        if i == 0:
            ring[ROWS + edge : ROWS + edge + 1, :] = ring[ROWS : ROWS + 1, :]
        ready = 0 if i == last else (parts if i == last - 1 else ((i + 1) * chunk - 1) // h)
        while done + 2 <= ready:
            for s in (done, done + 1):
                top, first = s * ROWS, ROWS + h * s
                for f in range(ROWS // h):
                    stage[top + f * h : top + (f + 1) * h, :core] = ring[first : first + h, f * core : (f + 1) * core]
                end = first - 1 if s % 2 == 0 else first + h
                for e in range(ROWS):
                    stage[top + e : top + e + 1, core : core + outer] = ring[end : end + 1, e * outer : (e + 1) * outer]
            both = slice(done * ROWS, (done + 2) * ROWS)
            out_ref[both, :] = stage[both, :].astype(jnp.bfloat16)
            done += 2


def own_kernel(h, columns, both_ref, out_ref):
    planes = 2 * h
    own = both_ref[...].astype(jnp.float32)
    for turn in range(2):
        for c in range(2):
            top = turn * planes + c * h
            for copy in range(ROWS // h):
                for m in range(columns):
                    out_ref[(turn * 2 + c) * columns + m, copy * h : (copy + 1) * h, :] = own[top : top + h, tile(m)]


def logits_kernel(
    edge, parts, total, orient_any, allowed_any, got_ref, own_ref, far_ref, out_ref, base_ref, bar_ref,
    orient_ref, allowed_ref, sems, x, z, far_flat, far_turned, wide_f32, flat, turned, kinds, shifted, gram,
):
    h = edge // parts
    wide = edge * edge
    columns = wide // LANES
    rows = total * h
    core, outer, extra = lanes_of(edge, parts)
    planes = 2 * h
    me = lax.axis_index("dp")
    scalars = [
        pltpu.make_async_copy(orient_any, orient_ref, sems.at[0]),
        pltpu.make_async_copy(allowed_any, allowed_ref, sems.at[1]),
    ]
    for copy in scalars:
        copy.start()
    low = lane_iota((ROWS, LANES)) < edge
    for j in range(extra // LANES):
        wide_f32[j] = got_ref[:, tile((core + outer) // LANES + j)].astype(jnp.float32)

    def keep(first, second, value, m):
        if planes == ROWS:
            upper = row_iota((ROWS, LANES)) < h
            other = pltpu.roll(value, h, 0)
            kinds[first * columns + m] = jnp.where(upper, value, other)
            kinds[second * columns + m] = jnp.where(upper, other, value)
        else:
            for number, kind in enumerate((first, second)):
                for copy in range(ROWS // h):
                    kinds[kind * columns + m, copy * h : (copy + 1) * h, :] = value[number * h : (number + 1) * h, :]

    for turn in range(2):
        for c in range(2):
            source, target = (turn * 2 + c) * columns, (turn * 4 + c) * columns
            kinds[target : target + columns] = own_ref[source : source + columns]
    for c in range(2):
        far = far_ref[c].astype(jnp.float32)
        for l in range(h):
            x[c * h + l : c * h + l + 1, :] = far[h - 1 - l : h - l, :]
    turn_rows(edge, planes, x, z, far_flat, far_turned)
    for m in range(columns):
        keep(2, 3, x[:planes, tile(m)], m)
        keep(6, 7, z[:planes, tile(m)], m)
    for axis in (1, 2):
        for c in range(2):
            for jl in range(h):
                first = (axis - 1) * 2 * h * edge // LANES
                for s in range(0, parts, ROWS):
                    tiles = [
                        wide_f32[first + i, pl.ds(s * ROWS + c * h + jl, ROWS, stride=ROWS), :] for i in range(h)
                    ]
                    for l in range(h):
                        plain, mirrored = tiles[l // 2], tiles[h // 2 + (h - 1 - l) // 2]
                        if l % 2 == 0:
                            value = jnp.where(low, plain, mirrored)
                        else:
                            value = swap_halves(jnp.where(low, mirrored, plain))
                        flat[pl.ds((c * h + l) * edge + s * h + jl, ROWS, stride=h), :] = value
        for l in range(h):
            block = jnp.concatenate(
                [flat[(c * h + l) * edge : (c * h + l + 1) * edge, :] for c in range(2)], axis=0
            ).T
            for side in range(2):
                turned[(side * h + l) * edge : (side * h + l + 1) * edge, :] = block[side * edge : (side + 1) * edge, :]
        part = lane_iota((planes, LANES)) < edge
        for m in range(edge // 2):
            even = flat[pl.ds(2 * m, planes, stride=edge), :]
            odd = flat[pl.ds(2 * m + 1, planes, stride=edge), :]
            keep(axis * 8, axis * 8 + 1, jnp.where(part, even, swap_halves(odd)), m)
            keep(axis * 8 + 2, axis * 8 + 3, jnp.where(part, swap_halves(even), odd), m)
            even = turned[pl.ds(2 * m, planes, stride=edge), :]
            odd = turned[pl.ds(2 * m + 1, planes, stride=edge), :]
            keep(axis * 8 + 4, axis * 8 + 6, jnp.where(part, even, swap_halves(odd)), m)
            keep(axis * 8 + 5, axis * 8 + 7, jnp.where(part, swap_halves(even), odd), m)
    for copy in scalars:
        copy.wait()
    lane = lane_iota((ROWS, LANES))
    slot = row_iota((ROWS, LANES)) // h
    per = ROWS // h
    lows = lane < edge
    after = (lane // edge) * edge + (lane + 1) % edge
    before = (lane // edge) * edge + (lane + edge - 1) % edge
    start, step, index = [], [], []
    for b in range(total // per):
        xor = jnp.zeros((ROWS, LANES), jnp.int32)
        for i in range(per):
            o = b * per + i
            turn = (orient_ref[o, 1] > orient_ref[o, 2]).astype(jnp.int32)
            kind = orient_ref[o, 0] * 8 + turn * 4 + orient_ref[o, 3] * 2 + o // ORI
            start.append(kind * columns + orient_ref[o, 4] * (columns - 1))
            step.append(1 - 2 * orient_ref[o, 4])
            xor = jnp.where(slot == i, orient_ref[o, 4] * edge + orient_ref[o, 5] * (edge - 1), xor)
        index.append([lane ^ xor, (lane ^ edge) ^ xor, before ^ xor, after ^ xor])

    def piece(o, j):
        return kinds[start[o] + j * step[o]]

    def column(j):
        found = []
        for b in range(total // per):
            value = piece(b * per, j)
            for i in range(1, per):
                value = jnp.where(slot == i, piece(b * per + i, j), value)
            found.append([pick_lanes(value, way) for way in index[b]])
        return [list(way) for way in zip(*found, strict=True)]

    behind = column(columns - 1)[1]
    here = column(0)
    for j in range(columns):
        ahead = column((j + 1) % columns)
        results = [
            here[0],
            [jnp.where(lows, x, y) for x, y in zip(behind, here[1], strict=True)],
            [jnp.where(lows, x, y) for x, y in zip(here[1], ahead[1], strict=True)],
            here[2],
            here[3],
        ]
        for number, result in enumerate(results):
            result = jnp.concatenate(result, axis=0).astype(jnp.bfloat16)
            shifted[number * rows : (number + 1) * rows, tile(j)] = result
            if number == 0:
                base_ref[:, tile(j)] = result
        behind, here = here[1], ahead
    many = parts * ROWS
    fraction = lane_iota((len(FLAT) * rows, many)) % ROWS // h
    found = None
    for f in range(ROWS // h):
        block = rows_by_rows(shifted[:, f * core : (f + 1) * core], got_ref[:, :core])
        found = block if found is None else jnp.where(fraction == f, block, found)
    gram[...] = found
    place = lane_iota((total, many)) % h
    kept = []
    for t, move in enumerate(MOVES):
        source = FLAT.index((move[1], move[2]))
        total_t = None
        for l in range(h):
            if many == LANES:
                block = gram[pl.ds(source * rows + l, total, stride=h), :]
            else:
                block = jnp.concatenate(
                    [gram[source * rows + o * h + l : source * rows + o * h + l + 1, :] for o in range(total)], axis=0
                )
            block = jnp.where(place == l + move[0], block, 0.0)
            total_t = block if total_t is None else total_t + block
        kept.append(total_t)
    if many == LANES:
        lane = lane_iota((total, LANES))
        result = jnp.zeros((total, LANES), jnp.float32)
        for t in range(len(MOVES)):
            value = kept[t]
            for step in (1, 2, 4):
                value = value + pltpu.roll(value, LANES - step, 1)
            result = jnp.where(lane // parts == t, pick_lanes(value, (lane % parts) * ROWS), result)
    else:
        shape = (len(MOVES) * many, SLOTS * parts)
        picker = (row_iota(shape) // ROWS == lane_iota(shape)).astype(jnp.float32)
        result = exactly(jnp.concatenate(kept, axis=1), picker)
    out_ref[...] = result
    kin = row_iota(result.shape) // ORI
    permit = jnp.zeros(result.shape, jnp.int32)
    for c in range(total // ORI):
        permit = jnp.where(kin == c, allowed_ref[0, c], permit)
    barred = (lane_iota(result.shape) % parts == me) & (permit != 1)
    bar_ref[...] = jnp.where(barred, jnp.float32(BARRED), jnp.float32(0.0))


def exactly(a, b):
    return jnp.dot(a, b, preferred_element_type=jnp.float32, precision=lax.Precision.HIGHEST)


def finish_kernel(
    h, parts, devices, scale, part_ref, base_ref, bar_ref, outer_ref, inner_ref, out_ref, ends
):
    me = lax.axis_index("dp")
    total = part_ref.shape[0]
    ends[:, : 2 * parts] = rows_by_rows(base_ref[...], jnp.concatenate([outer_ref[...], inner_ref[...]], axis=0))
    beyond = {1: (h - 1, parts * (1 - me % 2)), -1: (0, parts * (me % 2))}
    result = part_ref[...]
    lane = lane_iota(result.shape)
    for t, move in enumerate(MOVES):
        if not move[0]:
            continue
        l, left = beyond[move[0]]
        if result.shape[1] == LANES:
            value = pick_lanes(ends[pl.ds(l, total, stride=h), :], lane % parts + left)
            result = result + jnp.where(lane // parts == t, value, 0.0)
        else:
            shape = (2 * parts, SLOTS * parts)
            block = jnp.concatenate([ends[o * h + l : o * h + l + 1, : 2 * parts] for o in range(total)], axis=0)
            chosen = (row_iota(shape) == lane_iota(shape) % parts + left) & (lane_iota(shape) // parts == t)
            result = result + exactly(block, chosen.astype(jnp.float32))
    result = result * scale
    result = result + bar_ref[...]
    for d in range(devices):
        out_ref[d * total : (d + 1) * total, :] = result


def trim_kernel(edge, parts, got_ref, core_ref, outer_ref, lacking_ref):
    h = edge // parts
    core, outer, _ = lanes_of(edge, parts)
    core_ref[...] = got_ref[:, :core]
    whole = got_ref[:, core : core + outer].reshape(parts, ROWS, outer)
    for e in range(ROWS):
        outer_ref[:, e * outer : (e + 1) * outer] = whole[:, e, :]
    own_end(h, got_ref[:, :core].reshape(parts, ROWS, core), lacking_ref)


def own_end(h, whole, out_ref):
    core = whole.shape[2]
    even = lax.axis_index("dp") % 2 == 0

    @pl.when(even)
    def _():
        for f in range(ROWS // h):
            out_ref[:, f * core : (f + 1) * core] = whole[:, f * h + h - 1, :]

    @pl.when(jnp.logical_not(even))
    def _():
        for f in range(ROWS // h):
            out_ref[:, f * core : (f + 1) * core] = whole[:, f * h, :]


def far_ends_kernel(h, core_ref, out_ref, *tables):
    parts = core_ref.shape[0] // ROWS
    own_end(h, core_ref[...].reshape(parts, ROWS, core_ref.shape[1]), out_ref)
    for table in tables:
        many = parts * ROWS
        column = lane_iota(table.shape)
        particle = column % many // ROWS
        table[...] = (column // many * parts + particle == row_iota(table.shape)).astype(table.dtype)


def sums_kernel(edge, parts, total, groups, logits_ref, spread_ref, got_ref, *refs):
    pieces, refs = refs[: 3 * groups - 1], refs[3 * groups - 1 :]
    out_hbm, log_ref, out_ref, sems, in_sems, chances, weights, end_weights, table, merged, ends = refs
    h = edge // parts
    wide = edge * edge
    columns = wide // LANES
    owned = total // groups
    rows = owned * h
    span = SLOTS * parts
    many = parts * ROWS
    core, _, _ = lanes_of(edge, parts)
    mine, me = lax.axis_index("ref"), lax.axis_index("dp")
    incoming = []
    at_core, at_end = many, 0
    for number, piece in enumerate(pieces):
        if piece.shape[0] == many:
            target = merged.at[pl.ds(at_core, many)]
            at_core += many
        else:
            target = ends.at[pl.ds(at_end, parts)]
            at_end += parts
        incoming.append(pltpu.make_async_copy(piece, target, in_sems.at[number]))
        incoming[-1].start()
    merged[:many, :] = got_ref[:, :core]
    dot = functools.partial(jnp.dot, preferred_element_type=jnp.float32)
    lane = lane_iota((total, span))
    log_evidence = jnp.zeros((1, span), jnp.float32)
    for g in range(groups):
        scores = [logits_ref[(g * parts + s) * total : (g * parts + s + 1) * total, :] for s in range(parts)]
        while len(scores) > 1:
            scores = [sum(scores[i : i + 2]) for i in range(0, len(scores), 2)]
        score = jnp.where(lane >= len(MOVES) * parts, jnp.float32(-3e38), scores[0])
        peak = jnp.max(score, axis=0, keepdims=True)
        for step in (1, 2, 4):
            peak = jnp.maximum(peak, pltpu.roll(peak, step * parts, 1))
        expo = jnp.exp(score - peak)
        mass = jnp.sum(expo, axis=0, keepdims=True)
        for step in (1, 2, 4):
            mass = mass + pltpu.roll(mass, step * parts, 1)
        chances[g] = expo / mass
        log_evidence = jnp.where(mine == g, peak + jnp.log(mass), log_evidence)
    log_ref[...] = jnp.sum(jnp.where(lane_iota((1, span)) == me, log_evidence, 0.0), axis=1, keepdims=True)
    every = ends.shape[0]
    place, fraction = lane_iota((owned, many)) % h, lane_iota((owned, many)) % ROWS // h
    laid_ends = jnp.zeros((owned, 2 * every), jnp.float32)
    for k in range(groups):
        g = lax.rem(mine + groups - k, groups)
        if owned % ROWS == 0:
            chosen = chances[g, pl.ds(pl.multiple_of(mine * owned, ROWS), owned), :].astype(jnp.bfloat16)
        else:
            at = mine * owned + row_iota((owned, total))
            chooser = (at == lane_iota((owned, total))).astype(jnp.bfloat16)
            chosen = dot(chooser, chances[g].astype(jnp.bfloat16)).astype(jnp.bfloat16)
        laid = dot(chosen, spread_ref[...])
        for slot in range(len(FLAT)):
            for l in range(h):
                value = jnp.zeros((owned, many), jnp.float32)
                for t, move in enumerate(MOVES):
                    if FLAT.index((move[1], move[2])) == slot:
                        value = jnp.where(place == l + move[0], laid[:, t * many : (t + 1) * many], value)
                for f in range(ROWS // h):
                    part = jnp.where(fraction == f, value, 0.0)
                    for m in range(many // LANES):
                        at = (f * groups + k) * (many // LANES) + m
                        weights[at, pl.ds(slot * rows + l, owned, stride=h), :] = part[:, tile(m)]
        shape = (span, 2 * every)
        column = lane_iota(shape)
        up, down = MOVES.index((1, 0, 0)), MOVES.index((-1, 0, 0))
        shift = jnp.where(column < every, up, down)
        here = (column % every // (2 * parts) == k) & (row_iota(shape) == shift * parts + column % parts)
        laid_ends = laid_ends + dot(chosen, here.astype(jnp.bfloat16))
    side = lane_iota((owned, every)) % (2 * parts) // parts
    for l in range(h):
        value = jnp.zeros((owned, every), jnp.float32)
        if l == h - 1:
            value = value + jnp.where(side == 1 - me % 2, laid_ends[:, :every], 0.0)
        if l == 0:
            value = value + jnp.where(side == me % 2, laid_ends[:, every:], 0.0)
        if every < LANES:
            value = jnp.concatenate([value, jnp.zeros((owned, LANES - every), jnp.float32)], axis=1)
        for m in range(end_weights.shape[0]):
            end_weights[m, pl.ds(l, owned, stride=h), :] = value[:, tile(m)]
    for copy in incoming:
        copy.wait()
    count = groups * (many // LANES)
    for f in range(ROWS // h):
        both = jnp.concatenate([weights[f * count + m] for m in range(count)], axis=1).astype(jnp.bfloat16)
        table[:, f * core : (f + 1) * core] = dot(both, merged[...])
    both = jnp.concatenate([end_weights[m] for m in range(end_weights.shape[0])], axis=1)[:, :every]
    table[:rows, :] += dot(both.astype(jnp.bfloat16), ends[...])
    lane = lane_iota((rows, LANES))
    low = lane < edge
    after = (lane // edge) * edge + (lane + 1) % edge
    before = (lane // edge) * edge + (lane + edge - 1) % edge

    def cut(slot, j):
        return table[slot * rows : (slot + 1) * rows, tile(j % columns)]

    pieces = sems.shape[0]
    copies = []
    up = swap_halves(cut(1, 0))
    down = swap_halves(cut(2, columns - 1))
    for j in range(columns):
        up_next, down_next = swap_halves(cut(1, j + 1)), swap_halves(cut(2, j))
        value = cut(0, j) + jnp.where(low, up, up_next) + jnp.where(low, down, down_next)
        value = value + pick_lanes(cut(3, j), after) + pick_lanes(cut(4, j), before)
        up, down = up_next, down_next
        for o in range(owned):
            out_ref[o, :, tile(j)] = value[o * h : (o + 1) * h, :]
        if (j + 1) % (columns // pieces) == 0:
            number = len(copies)
            part = pl.ds(number * (wide // pieces), wide // pieces)
            copies.append(
                pltpu.make_async_copy(out_ref.at[:, :, part], out_hbm.at[:, :, part], sems.at[number])
            )
            copies[-1].start()
    for copy in copies:
        copy.wait()


def in_vmem():
    return pl.BlockSpec(memory_space=pltpu.VMEM)


def anywhere():
    return pl.BlockSpec(memory_space=pl.ANY)


def per_device(particles, references, orient, allowed):
    edge = particles.shape[1]
    wide = edge * edge
    total = orient.shape[0]
    parts = lax.axis_size("dp")
    groups = lax.axis_size("ref")
    devices = parts * groups
    h = edge // parts
    planes = 2 * h
    rows = total * h
    owned = total // groups
    span = SLOTS * parts
    core_lanes, _, extra = lanes_of(edge, parts)
    payload = sum(lanes_of(edge, parts))
    scale = 3.0 / math.sqrt(edge**3)
    params = pltpu.CompilerParams(vmem_limit_bytes=VMEM_BYTES)
    f32, bf16 = jnp.float32, jnp.bfloat16
    array = jax.ShapeDtypeStruct
    turning = [
        pltpu.VMEM((ROWS, wide), f32),
        pltpu.VMEM((ROWS, wide), f32),
        pltpu.VMEM((planes * edge, LANES), f32),
        pltpu.VMEM((planes * edge, LANES), f32),
    ]
    far = lax.ppermute(references, "dp", [(i, parts - 1 - i) for i in range(parts)])
    sent, both = pl.pallas_call(
        functools.partial(pack_kernel, edge, parts),
        out_shape=(array((parts * ROWS, payload), bf16), array((2 * planes, wide), bf16)),
        in_specs=[anywhere()] * 2,
        out_specs=(in_vmem(), in_vmem()),
        scratch_shapes=[
            pltpu.VMEM((edge, wide), bf16),
            pltpu.VMEM(references.shape, bf16),
            pltpu.SemaphoreType.DMA((1 + edge // (2 * ROWS),)),
            pltpu.VMEM((edge + 2 * ROWS, wide), f32),
            pltpu.VMEM((parts * ROWS, payload), f32),
            *turning,
        ],
        compiler_params=pltpu.CompilerParams(vmem_limit_bytes=MOST_VMEM),
        name="pack",
    )(particles.reshape(edge, wide), references)
    own = pl.pallas_call(
        functools.partial(own_kernel, h, wide // LANES),
        out_shape=array((4 * wide // LANES, ROWS, LANES), f32),
        in_specs=[in_vmem()],
        out_specs=in_vmem(),
        compiler_params=params,
        cost_estimate=pl.CostEstimate(flops=0, bytes_accessed=16 * 1024 * 1024, transcendentals=0),
        name="own",
    )(both)
    got = lax.all_to_all(sent, "dp", 0, 0, tiled=True)
    got, own, far = lax.optimization_barrier((got, own, far))
    plane = array((parts, wide), bf16)
    core, outer, lacking = pl.pallas_call(
        functools.partial(trim_kernel, edge, parts),
        out_shape=(array((parts * ROWS, core_lanes), bf16), plane, plane),
        in_specs=[in_vmem()],
        out_specs=(in_vmem(),) * 3,
        compiler_params=params,
        name="trim",
    )(got)
    pairs = [(i, i ^ 1) for i in range(parts)]
    inner = lax.ppermute(lacking, "dp", pairs)
    steps = [[(i, (i + k) % groups) for i in range(groups)] for k in range(1, groups)]
    cores = [lax.ppermute(core, "ref", step) for step in steps]
    partial, base, bars = pl.pallas_call(
        functools.partial(logits_kernel, edge, parts, total),
        out_shape=(array((total, span), f32), array((rows, wide), bf16), array((total, span), f32)),
        in_specs=[anywhere()] * 2 + [in_vmem()] * 3,
        out_specs=(in_vmem(),) * 3,
        scratch_shapes=[
            pltpu.SMEM(orient.shape, jnp.int32),
            pltpu.SMEM(allowed.shape, jnp.int32),
            pltpu.SemaphoreType.DMA((2,)),
            *turning,
            pltpu.VMEM((extra // LANES, parts * ROWS, LANES), f32),
            pltpu.VMEM((planes * edge, LANES), f32),
            pltpu.VMEM((planes * edge, LANES), f32),
            pltpu.VMEM((24 * wide // LANES, ROWS, LANES), f32),
            pltpu.VMEM((len(FLAT) * rows, wide), bf16),
            pltpu.VMEM((len(FLAT) * rows, parts * ROWS), f32),
        ],
        compiler_params=params,
        name="logits",
    )(orient, allowed, got, own, far)
    partial = pl.pallas_call(
        functools.partial(finish_kernel, h, parts, devices, scale),
        out_shape=array((devices * total, span), f32),
        in_specs=[in_vmem()] * 5,
        out_specs=in_vmem(),
        scratch_shapes=[pltpu.VMEM((rows, LANES), f32)],
        compiler_params=params,
        name="finish",
    )(partial, base, bars, outer, inner)
    partial, outside = lax.optimization_barrier((partial, outer))
    logits = lax.all_to_all(partial, ("ref", "dp"), 0, 0, tiled=True)
    tables = [array((span, len(MOVES) * parts * ROWS), bf16)]
    pieces = [outer, inner]
    for core, step in zip(cores, steps, strict=True):
        lacking, *laid = pl.pallas_call(
            functools.partial(far_ends_kernel, h),
            out_shape=(plane, *tables),
            in_specs=[in_vmem()],
            out_specs=(in_vmem(),) * (1 + len(tables)),
            compiler_params=params,
            cost_estimate=pl.CostEstimate(flops=0, bytes_accessed=16 * 1024 * 1024, transcendentals=0),
            name="far_ends",
        )(core)
        spread = laid[0] if laid else spread
        pieces += [core, lax.ppermute(outside, "ref", step), lax.ppermute(lacking, "dp", pairs)]
        tables = []
    every = groups * 2 * parts
    sums, log_evidence = pl.pallas_call(
        functools.partial(sums_kernel, edge, parts, total, groups),
        out_shape=(array((owned, h, wide), f32), array((1, 1), f32)),
        in_specs=[in_vmem()] * 3 + [anywhere()] * len(pieces),
        out_specs=(anywhere(), in_vmem()),
        scratch_shapes=[
            pltpu.VMEM((owned, h, wide), f32),
            pltpu.SemaphoreType.DMA((4,)),
            pltpu.SemaphoreType.DMA((len(pieces),)),
            pltpu.VMEM((groups, total, span), f32),
            pltpu.VMEM((ROWS // h * groups * parts * ROWS // LANES, len(FLAT) * owned * h, LANES), f32),
            pltpu.VMEM((max(every // LANES, 1), owned * h, LANES), f32),
            pltpu.VMEM((len(FLAT) * owned * h, wide), f32),
            pltpu.VMEM((groups * parts * ROWS, core_lanes), bf16),
            pltpu.VMEM((every, wide), bf16),
        ],
        compiler_params=params,
        name="sums",
    )(logits, spread, got, *pieces)
    return (sums, log_evidence.reshape(1))


def solution(mesh):
    return jax.shard_map(
        per_device,
        mesh=mesh,
        in_specs=(P(("ref", "dp"), None, None), P(None, "dp", None), P(), P(("ref", "dp"), None)),
        out_specs=(P("ref", "dp", None), P(("ref", "dp"))),
        check_vma=False,
    )
```

```python
import functools
import math

import jax
import jax.numpy as jnp
from jax import lax
from jax.experimental import pallas as pl
from jax.experimental.pallas import tpu as pltpu
from jax.sharding import PartitionSpec as P

ORI = 8
LANES = 128
ROWS = 8
MOVES = [(0, 0, 0), (1, 0, 0), (-1, 0, 0), (0, 1, 0), (0, -1, 0), (0, 0, 1), (0, 0, -1)]
FLAT = [(0, 0), (1, 0), (-1, 0), (0, 1), (0, -1)]
SLOTS = 8
BARRED = -1e30
VMEM_BYTES = 24 * 1024 * 1024
MOST_VMEM = 62 * 1024 * 1024


def lane_iota(shape):
    return lax.broadcasted_iota(jnp.int32, shape, len(shape) - 1)


def row_iota(shape):
    return lax.broadcasted_iota(jnp.int32, shape, 0)


def swap_halves(x):
    return pltpu.roll(x, LANES // 2, 1)


def rows_by_rows(a, b):
    return lax.dot_general(a, b, (((1,), (1,)), ((), ())), preferred_element_type=jnp.float32)


def pick_lanes(x, index):
    return jnp.take_along_axis(x, index, axis=1, mode="promise_in_bounds")


def tile(m):
    return slice(m * LANES, (m + 1) * LANES)


def lanes_of(edge, parts):
    h = edge // parts
    return edge * edge * h // ROWS, edge * edge // ROWS, 4 * h * edge


def turn_rows(edge, planes, x, z, flat, turned):
    lay_rows(edge, planes, x, flat)
    turn_planes(edge, planes, flat, turned)
    gather_rows(edge, planes, turned, z)


def lay_rows(edge, planes, x, flat):
    for m in range(edge // 2):
        piece = x[:planes, tile(m)]
        flat[pl.ds(2 * m, planes, stride=edge), :] = piece
        flat[pl.ds(2 * m + 1, planes, stride=edge), :] = swap_halves(piece)


def turn_planes(edge, planes, flat, turned):
    for n in range(0, planes, 2):
        block = flat[n * edge : (n + 2) * edge, :].T[:edge, :]
        turned[n * edge : (n + 1) * edge, :] = block
        turned[(n + 1) * edge : (n + 2) * edge, :] = swap_halves(block)


def gather_rows(edge, planes, turned, z):
    low = lane_iota((planes, LANES)) < edge
    for m in range(edge // 2):
        even = turned[pl.ds(2 * m, planes, stride=edge), :]
        odd = turned[pl.ds(2 * m + 1, planes, stride=edge), :]
        z[:planes, tile(m)] = jnp.where(low, even, swap_halves(odd))


def pack_kernel(
    edge, parts, part_hbm, refs_hbm, out_ref, both_ref, part_ref, refs_ref, sems, ring, stage, x, z, flat, turned
):
    h = edge // parts
    planes = 2 * h
    core, outer, _ = lanes_of(edge, parts)
    chunk = 2 * ROWS
    refs_copy = pltpu.make_async_copy(refs_hbm, refs_ref, sems.at[0])
    refs_copy.start()
    copies = []
    for i in range(edge // chunk):
        rows = pl.ds(i * chunk, chunk)
        copies.append(pltpu.make_async_copy(part_hbm.at[rows], part_ref.at[rows], sems.at[1 + i]))
        copies[-1].start()
    refs_copy.wait()
    for c in range(2):
        x[c * h : (c + 1) * h, :] = refs_ref[c].astype(jnp.float32)
    turn_rows(edge, planes, x, z, flat, turned)
    both_ref[...] = jnp.concatenate([x[:planes, :], z[:planes, :]], axis=0).astype(jnp.bfloat16)
    if planes < ROWS:
        stage[...] = jnp.zeros_like(stage)
    slab = h * edge
    for s in range(parts):
        top = s * ROWS
        mirror = parts - 1 - s
        for number, (array, place) in enumerate(((x, s), (x, mirror), (z, s), (z, mirror))):
            left = core + outer + number * slab
            stage[top : top + planes, left : left + slab] = array[:planes, place * slab : (place + 1) * slab]
    last = len(copies) - 1
    done = 0
    for i in [last] + list(range(last)):
        copies[i].wait()
        rows = slice(i * chunk, (i + 1) * chunk)
        ring[ROWS + i * chunk : ROWS + (i + 1) * chunk, :] = part_ref[rows, :].astype(jnp.float32)
        if i == last:
            ring[ROWS - 1 : ROWS, :] = ring[ROWS + edge - 1 : ROWS + edge, :]
        if i == 0:
            ring[ROWS + edge : ROWS + edge + 1, :] = ring[ROWS : ROWS + 1, :]
        ready = 0 if i == last else (parts if i == last - 1 else ((i + 1) * chunk - 1) // h)
        while done + 2 <= ready:
            for s in (done, done + 1):
                top, first = s * ROWS, ROWS + h * s
                for f in range(ROWS // h):
                    stage[top + f * h : top + (f + 1) * h, :core] = ring[first : first + h, f * core : (f + 1) * core]
                end = first - 1 if s % 2 == 0 else first + h
                for e in range(ROWS):
                    stage[top + e : top + e + 1, core : core + outer] = ring[end : end + 1, e * outer : (e + 1) * outer]
            both = slice(done * ROWS, (done + 2) * ROWS)
            out_ref[both, :] = stage[both, :].astype(jnp.bfloat16)
            done += 2


def own_kernel(h, columns, both_ref, out_ref):
    planes = 2 * h
    own = both_ref[...].astype(jnp.float32)
    for turn in range(2):
        for c in range(2):
            top = turn * planes + c * h
            for copy in range(ROWS // h):
                for m in range(columns):
                    out_ref[(turn * 2 + c) * columns + m, copy * h : (copy + 1) * h, :] = own[top : top + h, tile(m)]


def logits_kernel(
    edge, parts, total, orient_any, allowed_any, got_ref, own_ref, far_ref, out_ref, base_ref, bar_ref,
    orient_ref, allowed_ref, sems, x, z, far_flat, far_turned, wide_f32, flats, turneds, kinds, shifted, gram,
):
    h = edge // parts
    wide = edge * edge
    columns = wide // LANES
    rows = total * h
    core, outer, extra = lanes_of(edge, parts)
    planes = 2 * h
    me = lax.axis_index("dp")
    scalars = [
        pltpu.make_async_copy(orient_any, orient_ref, sems.at[0]),
        pltpu.make_async_copy(allowed_any, allowed_ref, sems.at[1]),
    ]
    for copy in scalars:
        copy.start()
    low = lane_iota((ROWS, LANES)) < edge
    for j in range(extra // LANES):
        wide_f32[j] = got_ref[:, tile((core + outer) // LANES + j)].astype(jnp.float32)

    def keep(first, second, value, m):
        if planes == ROWS:
            upper = row_iota((ROWS, LANES)) < h
            other = pltpu.roll(value, h, 0)
            kinds[first * columns + m] = jnp.where(upper, value, other)
            kinds[second * columns + m] = jnp.where(upper, other, value)
        else:
            for number, kind in enumerate((first, second)):
                for copy in range(ROWS // h):
                    kinds[kind * columns + m, copy * h : (copy + 1) * h, :] = value[number * h : (number + 1) * h, :]

    for turn in range(2):
        for c in range(2):
            source, target = (turn * 2 + c) * columns, (turn * 4 + c) * columns
            kinds[target : target + columns] = own_ref[source : source + columns]
    for c in range(2):
        far = far_ref[c].astype(jnp.float32)
        for l in range(h):
            x[c * h + l : c * h + l + 1, :] = far[h - 1 - l : h - l, :]
    lay_rows(edge, planes, x, far_flat)
    for axis in (1, 2):
        flat = flats.at[axis - 1]
        for c in range(2):
            for jl in range(h):
                first = (axis - 1) * 2 * h * edge // LANES
                for s in range(0, parts, ROWS):
                    tiles = [
                        wide_f32[first + i, pl.ds(s * ROWS + c * h + jl, ROWS, stride=ROWS), :] for i in range(h)
                    ]
                    for l in range(h):
                        plain, mirrored = tiles[l // 2], tiles[h // 2 + (h - 1 - l) // 2]
                        if l % 2 == 0:
                            value = jnp.where(low, plain, mirrored)
                        else:
                            value = swap_halves(jnp.where(low, mirrored, plain))
                        flat[pl.ds((c * h + l) * edge + s * h + jl, ROWS, stride=h), :] = value
    turn_planes(edge, planes, far_flat, far_turned)
    for axis in (1, 2):
        flat, turned = flats.at[axis - 1], turneds.at[axis - 1]
        for l in range(h):
            block = jnp.concatenate(
                [flat[(c * h + l) * edge : (c * h + l + 1) * edge, :] for c in range(2)], axis=0
            ).T
            for side in range(2):
                turned[(side * h + l) * edge : (side * h + l + 1) * edge, :] = block[side * edge : (side + 1) * edge, :]
    gather_rows(edge, planes, far_turned, z)
    for m in range(columns):
        keep(2, 3, x[:planes, tile(m)], m)
        keep(6, 7, z[:planes, tile(m)], m)
    for axis in (1, 2):
        flat, turned = flats.at[axis - 1], turneds.at[axis - 1]
        part = lane_iota((planes, LANES)) < edge
        for m in range(edge // 2):
            even = flat[pl.ds(2 * m, planes, stride=edge), :]
            odd = flat[pl.ds(2 * m + 1, planes, stride=edge), :]
            keep(axis * 8, axis * 8 + 1, jnp.where(part, even, swap_halves(odd)), m)
            keep(axis * 8 + 2, axis * 8 + 3, jnp.where(part, swap_halves(even), odd), m)
            even = turned[pl.ds(2 * m, planes, stride=edge), :]
            odd = turned[pl.ds(2 * m + 1, planes, stride=edge), :]
            keep(axis * 8 + 4, axis * 8 + 6, jnp.where(part, even, swap_halves(odd)), m)
            keep(axis * 8 + 5, axis * 8 + 7, jnp.where(part, swap_halves(even), odd), m)
    for copy in scalars:
        copy.wait()
    lane = lane_iota((ROWS, LANES))
    slot = row_iota((ROWS, LANES)) // h
    per = ROWS // h
    lows = lane < edge
    after = (lane // edge) * edge + (lane + 1) % edge
    before = (lane // edge) * edge + (lane + edge - 1) % edge
    start, step, index = [], [], []
    for b in range(total // per):
        xor = jnp.zeros((ROWS, LANES), jnp.int32)
        for i in range(per):
            o = b * per + i
            turn = (orient_ref[o, 1] > orient_ref[o, 2]).astype(jnp.int32)
            kind = orient_ref[o, 0] * 8 + turn * 4 + orient_ref[o, 3] * 2 + o // ORI
            start.append(kind * columns + orient_ref[o, 4] * (columns - 1))
            step.append(1 - 2 * orient_ref[o, 4])
            xor = jnp.where(slot == i, orient_ref[o, 4] * edge + orient_ref[o, 5] * (edge - 1), xor)
        index.append([lane ^ xor, (lane ^ edge) ^ xor, before ^ xor, after ^ xor])

    def piece(o, j):
        return kinds[start[o] + j * step[o]]

    def column(j):
        found = []
        for b in range(total // per):
            value = piece(b * per, j)
            for i in range(1, per):
                value = jnp.where(slot == i, piece(b * per + i, j), value)
            found.append([pick_lanes(value, way) for way in index[b]])
        return [list(way) for way in zip(*found, strict=True)]

    many = parts * ROWS
    fraction = lane_iota((len(FLAT) * rows, many)) % ROWS // h
    blocks = []

    def put(number, j, result):
        at = j % columns
        shifted[number * rows : (number + 1) * rows, tile(at)] = result
        if number == 0:
            base_ref[:, tile(at)] = result

    def joined(result):
        return jnp.concatenate(result, axis=0).astype(jnp.bfloat16)

    def between(first, second):
        return joined([jnp.where(lows, x, y) for x, y in zip(first[1], second[1], strict=True)])

    here = column(0)
    put(1, 0, between(column(columns - 1), here))
    for j in range(columns):
        ahead = column((j + 1) % columns)
        put(0, j, joined(here[0]))
        put(3, j, joined(here[2]))
        put(4, j, joined(here[3]))
        middle = between(here, ahead)
        put(2, j, middle)
        if j + 1 < columns:
            put(1, j + 1, middle)
        here = ahead
        f, rest = divmod((j + 1) * LANES, core)
        if rest == 0:
            blocks.append(rows_by_rows(shifted[:, (f - 1) * core : f * core], got_ref[:, :core]))
    found = blocks[0]
    for f in range(1, ROWS // h):
        found = jnp.where(fraction == f, blocks[f], found)
    gram[...] = found
    place = lane_iota((total, many)) % h
    kept = []
    for t, move in enumerate(MOVES):
        source = FLAT.index((move[1], move[2]))
        total_t = None
        for l in range(h):
            if many == LANES:
                block = gram[pl.ds(source * rows + l, total, stride=h), :]
            else:
                block = jnp.concatenate(
                    [gram[source * rows + o * h + l : source * rows + o * h + l + 1, :] for o in range(total)], axis=0
                )
            block = jnp.where(place == l + move[0], block, 0.0)
            total_t = block if total_t is None else total_t + block
        kept.append(total_t)
    if many == LANES:
        lane = lane_iota((total, LANES))
        result = jnp.zeros((total, LANES), jnp.float32)
        for t in range(len(MOVES)):
            value = kept[t]
            for step in (1, 2, 4):
                value = value + pltpu.roll(value, LANES - step, 1)
            result = jnp.where(lane // parts == t, pick_lanes(value, (lane % parts) * ROWS), result)
    else:
        shape = (len(MOVES) * many, SLOTS * parts)
        picker = (row_iota(shape) // ROWS == lane_iota(shape)).astype(jnp.float32)
        result = exactly(jnp.concatenate(kept, axis=1), picker)
    out_ref[...] = result
    kin = row_iota(result.shape) // ORI
    permit = jnp.zeros(result.shape, jnp.int32)
    for c in range(total // ORI):
        permit = jnp.where(kin == c, allowed_ref[0, c], permit)
    barred = (lane_iota(result.shape) % parts == me) & (permit != 1)
    bar_ref[...] = jnp.where(barred, jnp.float32(BARRED), jnp.float32(0.0))


def exactly(a, b):
    return jnp.dot(a, b, preferred_element_type=jnp.float32, precision=lax.Precision.HIGHEST)


def finish_kernel(
    h, parts, devices, scale, part_ref, base_ref, bar_ref, outer_ref, inner_ref, out_ref, ends
):
    me = lax.axis_index("dp")
    total = part_ref.shape[0]
    ends[:, : 2 * parts] = rows_by_rows(base_ref[...], jnp.concatenate([outer_ref[...], inner_ref[...]], axis=0))
    beyond = {1: (h - 1, parts * (1 - me % 2)), -1: (0, parts * (me % 2))}
    result = part_ref[...]
    lane = lane_iota(result.shape)
    for t, move in enumerate(MOVES):
        if not move[0]:
            continue
        l, left = beyond[move[0]]
        if result.shape[1] == LANES:
            value = pick_lanes(ends[pl.ds(l, total, stride=h), :], lane % parts + left)
            result = result + jnp.where(lane // parts == t, value, 0.0)
        else:
            shape = (2 * parts, SLOTS * parts)
            block = jnp.concatenate([ends[o * h + l : o * h + l + 1, : 2 * parts] for o in range(total)], axis=0)
            chosen = (row_iota(shape) == lane_iota(shape) % parts + left) & (lane_iota(shape) // parts == t)
            result = result + exactly(block, chosen.astype(jnp.float32))
    result = result * scale
    result = result + bar_ref[...]
    for d in range(devices):
        out_ref[d * total : (d + 1) * total, :] = result


def trim_kernel(edge, parts, got_ref, core_ref, outer_ref, lacking_ref):
    h = edge // parts
    core, outer, _ = lanes_of(edge, parts)
    core_ref[...] = got_ref[:, :core]
    whole = got_ref[:, core : core + outer].reshape(parts, ROWS, outer)
    for e in range(ROWS):
        outer_ref[:, e * outer : (e + 1) * outer] = whole[:, e, :]
    own_end(h, got_ref[:, :core].reshape(parts, ROWS, core), lacking_ref)


def own_end(h, whole, out_ref):
    core = whole.shape[2]
    even = lax.axis_index("dp") % 2 == 0

    @pl.when(even)
    def _():
        for f in range(ROWS // h):
            out_ref[:, f * core : (f + 1) * core] = whole[:, f * h + h - 1, :]

    @pl.when(jnp.logical_not(even))
    def _():
        for f in range(ROWS // h):
            out_ref[:, f * core : (f + 1) * core] = whole[:, f * h, :]


def far_ends_kernel(h, core_ref, out_ref, *tables):
    parts = core_ref.shape[0] // ROWS
    own_end(h, core_ref[...].reshape(parts, ROWS, core_ref.shape[1]), out_ref)
    for table in tables:
        many = parts * ROWS
        column = lane_iota(table.shape)
        particle = column % many // ROWS
        table[...] = (column // many * parts + particle == row_iota(table.shape)).astype(table.dtype)


def sums_kernel(edge, parts, total, groups, logits_ref, spread_ref, got_ref, *refs):
    pieces, refs = refs[: 3 * groups - 1], refs[3 * groups - 1 :]
    out_hbm, log_ref, out_ref, sems, chances, weights, end_weights, table, extra, merged, ends = refs
    h = edge // parts
    wide = edge * edge
    columns = wide // LANES
    owned = total // groups
    rows = owned * h
    span = SLOTS * parts
    many = parts * ROWS
    core, _, _ = lanes_of(edge, parts)
    mine, me = lax.axis_index("ref"), lax.axis_index("dp")
    at_core, at_end = many, 0
    for piece in pieces:
        if piece.shape[0] == many:
            merged[at_core : at_core + many, :] = piece[...]
            at_core += many
        else:
            ends[at_end : at_end + parts, :] = piece[...]
            at_end += parts
    merged[:many, :] = got_ref[:, :core]
    dot = functools.partial(jnp.dot, preferred_element_type=jnp.float32)
    lane = lane_iota((total, span))
    log_evidence = jnp.zeros((1, span), jnp.float32)
    for g in range(groups):
        scores = [logits_ref[(g * parts + s) * total : (g * parts + s + 1) * total, :] for s in range(parts)]
        while len(scores) > 1:
            scores = [sum(scores[i : i + 2]) for i in range(0, len(scores), 2)]
        score = jnp.where(lane >= len(MOVES) * parts, jnp.float32(-3e38), scores[0])
        peak = jnp.max(score, axis=0, keepdims=True)
        for step in (1, 2, 4):
            peak = jnp.maximum(peak, pltpu.roll(peak, step * parts, 1))
        expo = jnp.exp(score - peak)
        mass = jnp.sum(expo, axis=0, keepdims=True)
        for step in (1, 2, 4):
            mass = mass + pltpu.roll(mass, step * parts, 1)
        chances[g] = expo / mass
        log_evidence = jnp.where(mine == g, peak + jnp.log(mass), log_evidence)
    log_ref[...] = jnp.sum(jnp.where(lane_iota((1, span)) == me, log_evidence, 0.0), axis=1, keepdims=True)
    every = ends.shape[0]
    place, fraction = lane_iota((owned, many)) % h, lane_iota((owned, many)) % ROWS // h
    laid_ends = jnp.zeros((owned, 2 * every), jnp.float32)
    for k in range(groups):
        g = lax.rem(mine + groups - k, groups)
        if owned % ROWS == 0:
            chosen = chances[g, pl.ds(pl.multiple_of(mine * owned, ROWS), owned), :].astype(jnp.bfloat16)
        else:
            at = mine * owned + row_iota((owned, total))
            chooser = (at == lane_iota((owned, total))).astype(jnp.bfloat16)
            chosen = dot(chooser, chances[g].astype(jnp.bfloat16)).astype(jnp.bfloat16)
        laid = dot(chosen, spread_ref[...])
        for slot in range(len(FLAT)):
            for l in range(h):
                value = jnp.zeros((owned, many), jnp.float32)
                for t, move in enumerate(MOVES):
                    if FLAT.index((move[1], move[2])) == slot:
                        value = jnp.where(place == l + move[0], laid[:, t * many : (t + 1) * many], value)
                for f in range(ROWS // h):
                    part = jnp.where(fraction == f, value, 0.0)
                    for m in range(many // LANES):
                        at = (f * groups + k) * (many // LANES) + m
                        weights[at, pl.ds(slot * rows + l, owned, stride=h), :] = part[:, tile(m)]
        shape = (span, 2 * every)
        column = lane_iota(shape)
        up, down = MOVES.index((1, 0, 0)), MOVES.index((-1, 0, 0))
        shift = jnp.where(column < every, up, down)
        here = (column % every // (2 * parts) == k) & (row_iota(shape) == shift * parts + column % parts)
        laid_ends = laid_ends + dot(chosen, here.astype(jnp.bfloat16))
    side = lane_iota((owned, every)) % (2 * parts) // parts
    for l in range(h):
        value = jnp.zeros((owned, every), jnp.float32)
        if l == h - 1:
            value = value + jnp.where(side == 1 - me % 2, laid_ends[:, :every], 0.0)
        if l == 0:
            value = value + jnp.where(side == me % 2, laid_ends[:, every:], 0.0)
        if every < LANES:
            value = jnp.concatenate([value, jnp.zeros((owned, LANES - every), jnp.float32)], axis=1)
        for m in range(end_weights.shape[0]):
            end_weights[m, pl.ds(l, owned, stride=h), :] = value[:, tile(m)]
    count = groups * (many // LANES)
    for f in range(ROWS // h):
        both = jnp.concatenate([weights[f * count + m] for m in range(count)], axis=1).astype(jnp.bfloat16)
        table[:, f * core : (f + 1) * core] = dot(both, merged[...])
    both = jnp.concatenate([end_weights[m] for m in range(end_weights.shape[0])], axis=1)[:, :every]
    extra[...] = dot(both.astype(jnp.bfloat16), ends[...])
    lane = lane_iota((rows, LANES))
    low = lane < edge
    after = (lane // edge) * edge + (lane + 1) % edge
    before = (lane // edge) * edge + (lane + edge - 1) % edge

    def cut(slot, j):
        return table[slot * rows : (slot + 1) * rows, tile(j % columns)]

    pieces = sems.shape[0]
    copies = []
    for j in range(columns):
        turned = swap_halves(jnp.where(low, cut(1, j + 1) + cut(2, j), cut(1, j) + cut(2, j - 1)))
        value = cut(0, j) + extra[:, tile(j)] + turned
        value = value + pick_lanes(cut(3, j), after) + pick_lanes(cut(4, j), before)
        for o in range(owned):
            out_ref[o, :, tile(j)] = value[o * h : (o + 1) * h, :]
        if (j + 1) % (columns // pieces) == 0:
            number = len(copies)
            part = pl.ds(number * (wide // pieces), wide // pieces)
            copies.append(
                pltpu.make_async_copy(out_ref.at[:, :, part], out_hbm.at[:, :, part], sems.at[number])
            )
            copies[-1].start()
    for copy in copies:
        copy.wait()


def in_vmem():
    return pl.BlockSpec(memory_space=pltpu.VMEM)


def anywhere():
    return pl.BlockSpec(memory_space=pl.ANY)


def per_device(particles, references, orient, allowed):
    edge = particles.shape[1]
    wide = edge * edge
    total = orient.shape[0]
    parts = lax.axis_size("dp")
    groups = lax.axis_size("ref")
    devices = parts * groups
    h = edge // parts
    planes = 2 * h
    rows = total * h
    owned = total // groups
    span = SLOTS * parts
    core_lanes, _, extra = lanes_of(edge, parts)
    payload = sum(lanes_of(edge, parts))
    scale = 3.0 / math.sqrt(edge**3)
    params = pltpu.CompilerParams(vmem_limit_bytes=VMEM_BYTES)
    f32, bf16 = jnp.float32, jnp.bfloat16
    array = jax.ShapeDtypeStruct
    turning = [
        pltpu.VMEM((ROWS, wide), f32),
        pltpu.VMEM((ROWS, wide), f32),
        pltpu.VMEM((planes * edge, LANES), f32),
        pltpu.VMEM((planes * edge, LANES), f32),
    ]
    far = lax.ppermute(references, "dp", [(i, parts - 1 - i) for i in range(parts)])
    sent, both = pl.pallas_call(
        functools.partial(pack_kernel, edge, parts),
        out_shape=(array((parts * ROWS, payload), bf16), array((2 * planes, wide), bf16)),
        in_specs=[anywhere()] * 2,
        out_specs=(in_vmem(), in_vmem()),
        scratch_shapes=[
            pltpu.VMEM((edge, wide), bf16),
            pltpu.VMEM(references.shape, bf16),
            pltpu.SemaphoreType.DMA((1 + edge // (2 * ROWS),)),
            pltpu.VMEM((edge + 2 * ROWS, wide), f32),
            pltpu.VMEM((parts * ROWS, payload), f32),
            *turning,
        ],
        compiler_params=pltpu.CompilerParams(vmem_limit_bytes=MOST_VMEM),
        name="pack",
    )(particles.reshape(edge, wide), references)
    own = pl.pallas_call(
        functools.partial(own_kernel, h, wide // LANES),
        out_shape=array((4 * wide // LANES, ROWS, LANES), f32),
        in_specs=[in_vmem()],
        out_specs=in_vmem(),
        compiler_params=params,
        cost_estimate=pl.CostEstimate(flops=0, bytes_accessed=16 * 1024 * 1024, transcendentals=0),
        name="own",
    )(both)
    got = lax.all_to_all(sent, "dp", 0, 0, tiled=True)
    got, own, far = lax.optimization_barrier((got, own, far))
    plane = array((parts, wide), bf16)
    core, outer, lacking = pl.pallas_call(
        functools.partial(trim_kernel, edge, parts),
        out_shape=(array((parts * ROWS, core_lanes), bf16), plane, plane),
        in_specs=[in_vmem()],
        out_specs=(in_vmem(),) * 3,
        compiler_params=params,
        name="trim",
    )(got)
    pairs = [(i, i ^ 1) for i in range(parts)]
    inner = lax.ppermute(lacking, "dp", pairs)
    steps = [[(i, (i + k) % groups) for i in range(groups)] for k in range(1, groups)]
    cores = [lax.ppermute(core, "ref", step) for step in steps]
    partial, base, bars = pl.pallas_call(
        functools.partial(logits_kernel, edge, parts, total),
        out_shape=(array((total, span), f32), array((rows, wide), bf16), array((total, span), f32)),
        in_specs=[anywhere()] * 2 + [in_vmem()] * 3,
        out_specs=(in_vmem(),) * 3,
        scratch_shapes=[
            pltpu.SMEM(orient.shape, jnp.int32),
            pltpu.SMEM(allowed.shape, jnp.int32),
            pltpu.SemaphoreType.DMA((2,)),
            *turning,
            pltpu.VMEM((extra // LANES, parts * ROWS, LANES), f32),
            pltpu.VMEM((2, planes * edge, LANES), f32),
            pltpu.VMEM((2, planes * edge, LANES), f32),
            pltpu.VMEM((24 * wide // LANES, ROWS, LANES), f32),
            pltpu.VMEM((len(FLAT) * rows, wide), bf16),
            pltpu.VMEM((len(FLAT) * rows, parts * ROWS), f32),
        ],
        compiler_params=params,
        name="logits",
    )(orient, allowed, got, own, far)
    partial = pl.pallas_call(
        functools.partial(finish_kernel, h, parts, devices, scale),
        out_shape=array((devices * total, span), f32),
        in_specs=[in_vmem()] * 5,
        out_specs=in_vmem(),
        scratch_shapes=[pltpu.VMEM((rows, LANES), f32)],
        compiler_params=params,
        name="finish",
    )(partial, base, bars, outer, inner)
    partial, outside = lax.optimization_barrier((partial, outer))
    logits = lax.all_to_all(partial, ("ref", "dp"), 0, 0, tiled=True)
    tables = [array((span, len(MOVES) * parts * ROWS), bf16)]
    pieces = [outer, inner]
    for core, step in zip(cores, steps, strict=True):
        lacking, *laid = pl.pallas_call(
            functools.partial(far_ends_kernel, h),
            out_shape=(plane, *tables),
            in_specs=[in_vmem()],
            out_specs=(in_vmem(),) * (1 + len(tables)),
            compiler_params=params,
            cost_estimate=pl.CostEstimate(flops=0, bytes_accessed=16 * 1024 * 1024, transcendentals=0),
            name="far_ends",
        )(core)
        spread = laid[0] if laid else spread
        pieces += [core, lax.ppermute(outside, "ref", step), lax.ppermute(lacking, "dp", pairs)]
        tables = []
    every = groups * 2 * parts
    sums, log_evidence = pl.pallas_call(
        functools.partial(sums_kernel, edge, parts, total, groups),
        out_shape=(array((owned, h, wide), f32), array((1, 1), f32)),
        in_specs=[in_vmem()] * (3 + len(pieces)),
        out_specs=(anywhere(), in_vmem()),
        scratch_shapes=[
            pltpu.VMEM((owned, h, wide), f32),
            pltpu.SemaphoreType.DMA((8,)),
            pltpu.VMEM((groups, total, span), f32),
            pltpu.VMEM((ROWS // h * groups * parts * ROWS // LANES, len(FLAT) * owned * h, LANES), f32),
            pltpu.VMEM((max(every // LANES, 1), owned * h, LANES), f32),
            pltpu.VMEM((len(FLAT) * owned * h, wide), f32),
            pltpu.VMEM((owned * h, wide), f32),
            pltpu.VMEM((groups * parts * ROWS, core_lanes), bf16),
            pltpu.VMEM((every, wide), bf16),
        ],
        compiler_params=params,
        name="sums",
    )(logits, spread, got, *pieces)
    return (sums, log_evidence.reshape(1))


def solution(mesh):
    return jax.shard_map(
        per_device,
        mesh=mesh,
        in_specs=(P(("ref", "dp"), None, None), P(None, "dp", None), P(), P(("ref", "dp"), None)),
        out_specs=(P("ref", "dp", None), P(("ref", "dp"))),
        check_vma=False,
    )
```

```python
import functools
import math

import jax
import jax.numpy as jnp
from jax import lax
from jax.experimental import pallas as pl
from jax.experimental.pallas import tpu as pltpu
from jax.sharding import PartitionSpec as P

ORI = 8
LANES = 128
ROWS = 8
MOVES = [(0, 0, 0), (1, 0, 0), (-1, 0, 0), (0, 1, 0), (0, -1, 0), (0, 0, 1), (0, 0, -1)]
FLAT = [(0, 0), (1, 0), (-1, 0), (0, 1), (0, -1)]
SLOTS = 8
BARRED = -1e30
VMEM_BYTES = 24 * 1024 * 1024
MOST_VMEM = 62 * 1024 * 1024


def lane_iota(shape):
    return lax.broadcasted_iota(jnp.int32, shape, len(shape) - 1)


def row_iota(shape):
    return lax.broadcasted_iota(jnp.int32, shape, 0)


def swap_halves(x):
    return pltpu.roll(x, LANES // 2, 1)


def rows_by_rows(a, b):
    return lax.dot_general(a, b, (((1,), (1,)), ((), ())), preferred_element_type=jnp.float32)


def pick_lanes(x, index):
    return jnp.take_along_axis(x, index, axis=1, mode="promise_in_bounds")


def tile(m):
    return slice(m * LANES, (m + 1) * LANES)


def lanes_of(edge, parts):
    h = edge // parts
    return edge * edge * h // ROWS, edge * edge // ROWS, 4 * h * edge


def turn_rows(edge, planes, x, z, flat, turned):
    lay_rows(edge, planes, x, flat)
    turn_planes(edge, planes, flat, turned)
    gather_rows(edge, planes, turned, z)


def lay_rows(edge, planes, x, flat):
    for m in range(edge // 2):
        piece = x[:planes, tile(m)]
        flat[pl.ds(2 * m, planes, stride=edge), :] = piece
        flat[pl.ds(2 * m + 1, planes, stride=edge), :] = swap_halves(piece)


def turn_planes(edge, planes, flat, turned):
    for n in range(0, planes, 2):
        block = flat[n * edge : (n + 2) * edge, :].T[:edge, :]
        turned[n * edge : (n + 1) * edge, :] = block
        turned[(n + 1) * edge : (n + 2) * edge, :] = swap_halves(block)


def gather_rows(edge, planes, turned, z):
    low = lane_iota((planes, LANES)) < edge
    for m in range(edge // 2):
        even = turned[pl.ds(2 * m, planes, stride=edge), :]
        odd = turned[pl.ds(2 * m + 1, planes, stride=edge), :]
        z[:planes, tile(m)] = jnp.where(low, even, swap_halves(odd))


def pack_kernel(
    edge, parts, part_hbm, refs_hbm, out_ref, both_ref, part_ref, refs_ref, sems, ring, stage, x, z, flat, turned
):
    h = edge // parts
    planes = 2 * h
    core, outer, _ = lanes_of(edge, parts)
    chunk = 2 * ROWS
    refs_copy = pltpu.make_async_copy(refs_hbm, refs_ref, sems.at[0])
    refs_copy.start()
    copies = []
    for i in range(edge // chunk):
        rows = pl.ds(i * chunk, chunk)
        copies.append(pltpu.make_async_copy(part_hbm.at[rows], part_ref.at[rows], sems.at[1 + i]))
        copies[-1].start()
    refs_copy.wait()
    for c in range(2):
        x[c * h : (c + 1) * h, :] = refs_ref[c].astype(jnp.float32)
    turn_rows(edge, planes, x, z, flat, turned)
    both_ref[...] = jnp.concatenate([x[:planes, :], z[:planes, :]], axis=0).astype(jnp.bfloat16)
    if planes < ROWS:
        stage[...] = jnp.zeros_like(stage)
    slab = h * edge
    for s in range(parts):
        top = s * ROWS
        mirror = parts - 1 - s
        for number, (array, place) in enumerate(((x, s), (x, mirror), (z, s), (z, mirror))):
            left = core + outer + number * slab
            stage[top : top + planes, left : left + slab] = array[:planes, place * slab : (place + 1) * slab]
    last = len(copies) - 1
    done = 0
    for i in [last] + list(range(last)):
        copies[i].wait()
        rows = slice(i * chunk, (i + 1) * chunk)
        ring[ROWS + i * chunk : ROWS + (i + 1) * chunk, :] = part_ref[rows, :].astype(jnp.float32)
        if i == last:
            ring[ROWS - 1 : ROWS, :] = ring[ROWS + edge - 1 : ROWS + edge, :]
        if i == 0:
            ring[ROWS + edge : ROWS + edge + 1, :] = ring[ROWS : ROWS + 1, :]
        ready = 0 if i == last else (parts if i == last - 1 else ((i + 1) * chunk - 1) // h)
        while done + 2 <= ready:
            for s in (done, done + 1):
                top, first = s * ROWS, ROWS + h * s
                for f in range(ROWS // h):
                    stage[top + f * h : top + (f + 1) * h, :core] = ring[first : first + h, f * core : (f + 1) * core]
                end = first - 1 if s % 2 == 0 else first + h
                for e in range(ROWS):
                    stage[top + e : top + e + 1, core : core + outer] = ring[end : end + 1, e * outer : (e + 1) * outer]
            both = slice(done * ROWS, (done + 2) * ROWS)
            out_ref[both, :] = stage[both, :].astype(jnp.bfloat16)
            done += 2


def own_kernel(h, columns, both_ref, out_ref):
    planes = 2 * h
    own = both_ref[...].astype(jnp.float32)
    for turn in range(2):
        for c in range(2):
            top = turn * planes + c * h
            for copy in range(ROWS // h):
                for m in range(columns):
                    out_ref[(turn * 2 + c) * columns + m, copy * h : (copy + 1) * h, :] = own[top : top + h, tile(m)]


def logits_kernel(
    edge, parts, total, orient_any, allowed_any, got_ref, own_ref, far_ref, out_ref, base_ref, bar_ref,
    orient_ref, allowed_ref, sems, x, z, far_flat, far_turned, wide_f32, flats, turneds, kinds, shifted, gram,
):
    h = edge // parts
    wide = edge * edge
    columns = wide // LANES
    rows = total * h
    core, outer, extra = lanes_of(edge, parts)
    planes = 2 * h
    me = lax.axis_index("dp")
    scalars = [
        pltpu.make_async_copy(orient_any, orient_ref, sems.at[0]),
        pltpu.make_async_copy(allowed_any, allowed_ref, sems.at[1]),
    ]
    for copy in scalars:
        copy.start()
    low = lane_iota((ROWS, LANES)) < edge
    for j in range(extra // LANES):
        wide_f32[j] = got_ref[:, tile((core + outer) // LANES + j)].astype(jnp.float32)

    def keep(first, second, value, m):
        if planes == ROWS:
            upper = row_iota((ROWS, LANES)) < h
            other = pltpu.roll(value, h, 0)
            kinds[first * columns + m] = jnp.where(upper, value, other)
            kinds[second * columns + m] = jnp.where(upper, other, value)
        else:
            for number, kind in enumerate((first, second)):
                for copy in range(ROWS // h):
                    kinds[kind * columns + m, copy * h : (copy + 1) * h, :] = value[number * h : (number + 1) * h, :]

    for turn in range(2):
        for c in range(2):
            source, target = (turn * 2 + c) * columns, (turn * 4 + c) * columns
            kinds[target : target + columns] = own_ref[source : source + columns]
    for c in range(2):
        far = far_ref[c].astype(jnp.float32)
        for l in range(h):
            x[c * h + l : c * h + l + 1, :] = far[h - 1 - l : h - l, :]
    lay_rows(edge, planes, x, far_flat)
    for axis in (1, 2):
        flat = flats.at[axis - 1]
        for c in range(2):
            for jl in range(h):
                first = (axis - 1) * 2 * h * edge // LANES
                for s in range(0, parts, ROWS):
                    tiles = [
                        wide_f32[first + i, pl.ds(s * ROWS + c * h + jl, ROWS, stride=ROWS), :] for i in range(h)
                    ]
                    for l in range(h):
                        plain, mirrored = tiles[l // 2], tiles[h // 2 + (h - 1 - l) // 2]
                        if l % 2 == 0:
                            value = jnp.where(low, plain, mirrored)
                        else:
                            value = swap_halves(jnp.where(low, mirrored, plain))
                        flat[pl.ds((c * h + l) * edge + s * h + jl, ROWS, stride=h), :] = value
    turn_planes(edge, planes, far_flat, far_turned)
    for axis in (1, 2):
        flat, turned = flats.at[axis - 1], turneds.at[axis - 1]
        for l in range(h):
            block = jnp.concatenate(
                [flat[(c * h + l) * edge : (c * h + l + 1) * edge, :] for c in range(2)], axis=0
            ).T
            for side in range(2):
                turned[(side * h + l) * edge : (side * h + l + 1) * edge, :] = block[side * edge : (side + 1) * edge, :]
    gather_rows(edge, planes, far_turned, z)
    for m in range(columns):
        keep(2, 3, x[:planes, tile(m)], m)
        keep(6, 7, z[:planes, tile(m)], m)
    for axis in (1, 2):
        flat, turned = flats.at[axis - 1], turneds.at[axis - 1]
        part = lane_iota((planes, LANES)) < edge
        for m in range(edge // 2):
            even = flat[pl.ds(2 * m, planes, stride=edge), :]
            odd = flat[pl.ds(2 * m + 1, planes, stride=edge), :]
            keep(axis * 8, axis * 8 + 1, jnp.where(part, even, swap_halves(odd)), m)
            keep(axis * 8 + 2, axis * 8 + 3, jnp.where(part, swap_halves(even), odd), m)
            even = turned[pl.ds(2 * m, planes, stride=edge), :]
            odd = turned[pl.ds(2 * m + 1, planes, stride=edge), :]
            keep(axis * 8 + 4, axis * 8 + 6, jnp.where(part, even, swap_halves(odd)), m)
            keep(axis * 8 + 5, axis * 8 + 7, jnp.where(part, swap_halves(even), odd), m)
    for copy in scalars:
        copy.wait()
    lane = lane_iota((ROWS, LANES))
    slot = row_iota((ROWS, LANES)) // h
    per = ROWS // h
    lows = lane < edge
    after = (lane // edge) * edge + (lane + 1) % edge
    before = (lane // edge) * edge + (lane + edge - 1) % edge
    start, step, index = [], [], []
    for b in range(total // per):
        xor = jnp.zeros((ROWS, LANES), jnp.int32)
        for i in range(per):
            o = b * per + i
            turn = (orient_ref[o, 1] > orient_ref[o, 2]).astype(jnp.int32)
            kind = orient_ref[o, 0] * 8 + turn * 4 + orient_ref[o, 3] * 2 + o // ORI
            start.append(kind * columns + orient_ref[o, 4] * (columns - 1))
            step.append(1 - 2 * orient_ref[o, 4])
            xor = jnp.where(slot == i, orient_ref[o, 4] * edge + orient_ref[o, 5] * (edge - 1), xor)
        index.append([lane ^ xor, (lane ^ edge) ^ xor, before ^ xor, after ^ xor])

    def piece(o, j):
        return kinds[start[o] + j * step[o]]

    def column(j):
        found = []
        for b in range(total // per):
            value = piece(b * per, j)
            for i in range(1, per):
                value = jnp.where(slot == i, piece(b * per + i, j), value)
            found.append([pick_lanes(value, way) for way in index[b]])
        return [list(way) for way in zip(*found, strict=True)]

    many = parts * ROWS
    fraction = lane_iota((len(FLAT) * rows, many)) % ROWS // h
    blocks = []

    def put(number, j, result):
        at = j % columns
        shifted[number * rows : (number + 1) * rows, tile(at)] = result
        if number == 0:
            base_ref[:, tile(at)] = result

    def joined(result):
        return jnp.concatenate(result, axis=0).astype(jnp.bfloat16)

    def between(first, second):
        return joined([jnp.where(lows, x, y) for x, y in zip(first[1], second[1], strict=True)])

    here = column(0)
    put(1, 0, between(column(columns - 1), here))
    for j in range(columns):
        ahead = column((j + 1) % columns)
        put(0, j, joined(here[0]))
        put(3, j, joined(here[2]))
        put(4, j, joined(here[3]))
        middle = between(here, ahead)
        put(2, j, middle)
        if j + 1 < columns:
            put(1, j + 1, middle)
        here = ahead
        f, rest = divmod((j + 1) * LANES, core)
        if rest == 0:
            blocks.append(rows_by_rows(shifted[:, (f - 1) * core : f * core], got_ref[:, :core]))
    found = blocks[0]
    for f in range(1, ROWS // h):
        found = jnp.where(fraction == f, blocks[f], found)
    gram[...] = found
    place = lane_iota((total, many)) % h
    kept = []
    for t, move in enumerate(MOVES):
        source = FLAT.index((move[1], move[2]))
        total_t = None
        for l in range(h):
            if many == LANES:
                block = gram[pl.ds(source * rows + l, total, stride=h), :]
            else:
                block = jnp.concatenate(
                    [gram[source * rows + o * h + l : source * rows + o * h + l + 1, :] for o in range(total)], axis=0
                )
            block = jnp.where(place == l + move[0], block, 0.0)
            total_t = block if total_t is None else total_t + block
        kept.append(total_t)
    if many == LANES:
        lane = lane_iota((total, LANES))
        result = jnp.zeros((total, LANES), jnp.float32)
        for t in range(len(MOVES)):
            value = kept[t]
            for step in (1, 2, 4):
                value = value + pltpu.roll(value, LANES - step, 1)
            result = jnp.where(lane // parts == t, pick_lanes(value, (lane % parts) * ROWS), result)
    else:
        shape = (len(MOVES) * many, SLOTS * parts)
        picker = (row_iota(shape) // ROWS == lane_iota(shape)).astype(jnp.float32)
        result = exactly(jnp.concatenate(kept, axis=1), picker)
    out_ref[...] = result
    kin = row_iota(result.shape) // ORI
    permit = jnp.zeros(result.shape, jnp.int32)
    for c in range(total // ORI):
        permit = jnp.where(kin == c, allowed_ref[0, c], permit)
    barred = (lane_iota(result.shape) % parts == me) & (permit != 1)
    bar_ref[...] = jnp.where(barred, jnp.float32(BARRED), jnp.float32(0.0))


def exactly(a, b):
    return jnp.dot(a, b, preferred_element_type=jnp.float32, precision=lax.Precision.HIGHEST)


def finish_kernel(
    h, parts, devices, scale, part_ref, base_ref, bar_ref, outer_ref, inner_ref, out_ref, ends
):
    me = lax.axis_index("dp")
    total = part_ref.shape[0]
    ends[:, : 2 * parts] = rows_by_rows(base_ref[...], jnp.concatenate([outer_ref[...], inner_ref[...]], axis=0))
    beyond = {1: (h - 1, parts * (1 - me % 2)), -1: (0, parts * (me % 2))}
    result = part_ref[...]
    lane = lane_iota(result.shape)
    for t, move in enumerate(MOVES):
        if not move[0]:
            continue
        l, left = beyond[move[0]]
        if result.shape[1] == LANES:
            value = pick_lanes(ends[pl.ds(l, total, stride=h), :], lane % parts + left)
            result = result + jnp.where(lane // parts == t, value, 0.0)
        else:
            shape = (2 * parts, SLOTS * parts)
            block = jnp.concatenate([ends[o * h + l : o * h + l + 1, : 2 * parts] for o in range(total)], axis=0)
            chosen = (row_iota(shape) == lane_iota(shape) % parts + left) & (lane_iota(shape) // parts == t)
            result = result + exactly(block, chosen.astype(jnp.float32))
    result = result * scale
    result = result + bar_ref[...]
    for d in range(devices):
        out_ref[d * total : (d + 1) * total, :] = result


def trim_kernel(edge, parts, got_ref, core_ref, outer_ref, lacking_ref):
    h = edge // parts
    core, outer, _ = lanes_of(edge, parts)
    core_ref[...] = got_ref[:, :core]
    whole = got_ref[:, core : core + outer].reshape(parts, ROWS, outer)
    for e in range(ROWS):
        outer_ref[:, e * outer : (e + 1) * outer] = whole[:, e, :]
    own_end(h, got_ref[:, :core].reshape(parts, ROWS, core), lacking_ref)


def own_end(h, whole, out_ref):
    core = whole.shape[2]
    even = lax.axis_index("dp") % 2 == 0

    @pl.when(even)
    def _():
        for f in range(ROWS // h):
            out_ref[:, f * core : (f + 1) * core] = whole[:, f * h + h - 1, :]

    @pl.when(jnp.logical_not(even))
    def _():
        for f in range(ROWS // h):
            out_ref[:, f * core : (f + 1) * core] = whole[:, f * h, :]


def far_ends_kernel(h, core_ref, out_ref, *tables):
    parts = core_ref.shape[0] // ROWS
    own_end(h, core_ref[...].reshape(parts, ROWS, core_ref.shape[1]), out_ref)
    for table in tables:
        many = parts * ROWS
        column = lane_iota(table.shape)
        particle = column % many // ROWS
        table[...] = (column // many * parts + particle == row_iota(table.shape)).astype(table.dtype)


def sums_kernel(edge, parts, total, groups, logits_ref, spread_ref, got_ref, *refs):
    pieces, refs = refs[: 3 * groups - 1], refs[3 * groups - 1 :]
    out_ref, log_ref, chances, weights, end_weights, table, extra, merged, ends = refs
    h = edge // parts
    wide = edge * edge
    columns = wide // LANES
    owned = total // groups
    rows = owned * h
    span = SLOTS * parts
    many = parts * ROWS
    core, _, _ = lanes_of(edge, parts)
    mine, me = lax.axis_index("ref"), lax.axis_index("dp")
    at_core, at_end = many, 0
    for piece in pieces:
        if piece.shape[0] == many:
            merged[at_core : at_core + many, :] = piece[...]
            at_core += many
        else:
            ends[at_end : at_end + parts, :] = piece[...]
            at_end += parts
    merged[:many, :] = got_ref[:, :core]
    dot = functools.partial(jnp.dot, preferred_element_type=jnp.float32)
    lane = lane_iota((total, span))
    log_evidence = jnp.zeros((1, span), jnp.float32)
    for g in range(groups):
        scores = [logits_ref[(g * parts + s) * total : (g * parts + s + 1) * total, :] for s in range(parts)]
        while len(scores) > 1:
            scores = [sum(scores[i : i + 2]) for i in range(0, len(scores), 2)]
        score = jnp.where(lane >= len(MOVES) * parts, jnp.float32(-3e38), scores[0])
        peak = jnp.max(score, axis=0, keepdims=True)
        for step in (1, 2, 4):
            peak = jnp.maximum(peak, pltpu.roll(peak, step * parts, 1))
        expo = jnp.exp(score - peak)
        mass = jnp.sum(expo, axis=0, keepdims=True)
        for step in (1, 2, 4):
            mass = mass + pltpu.roll(mass, step * parts, 1)
        chances[g] = expo / mass
        log_evidence = jnp.where(mine == g, peak + jnp.log(mass), log_evidence)
    log_ref[...] = jnp.sum(jnp.where(lane_iota((1, span)) == me, log_evidence, 0.0), axis=1, keepdims=True)
    every = ends.shape[0]
    place, fraction = lane_iota((owned, many)) % h, lane_iota((owned, many)) % ROWS // h
    laid_ends = jnp.zeros((owned, 2 * every), jnp.float32)
    for k in range(groups):
        g = lax.rem(mine + groups - k, groups)
        if owned % ROWS == 0:
            chosen = chances[g, pl.ds(pl.multiple_of(mine * owned, ROWS), owned), :].astype(jnp.bfloat16)
        else:
            at = mine * owned + row_iota((owned, total))
            chooser = (at == lane_iota((owned, total))).astype(jnp.bfloat16)
            chosen = dot(chooser, chances[g].astype(jnp.bfloat16)).astype(jnp.bfloat16)
        laid = dot(chosen, spread_ref[...])
        for slot in range(len(FLAT)):
            for l in range(h):
                value = jnp.zeros((owned, many), jnp.float32)
                for t, move in enumerate(MOVES):
                    if FLAT.index((move[1], move[2])) == slot:
                        value = jnp.where(place == l + move[0], laid[:, t * many : (t + 1) * many], value)
                for f in range(ROWS // h):
                    part = jnp.where(fraction == f, value, 0.0)
                    for m in range(many // LANES):
                        at = (f * groups + k) * (many // LANES) + m
                        weights[at, pl.ds(slot * rows + l, owned, stride=h), :] = part[:, tile(m)]
        shape = (span, 2 * every)
        column = lane_iota(shape)
        up, down = MOVES.index((1, 0, 0)), MOVES.index((-1, 0, 0))
        shift = jnp.where(column < every, up, down)
        here = (column % every // (2 * parts) == k) & (row_iota(shape) == shift * parts + column % parts)
        laid_ends = laid_ends + dot(chosen, here.astype(jnp.bfloat16))
    side = lane_iota((owned, every)) % (2 * parts) // parts
    for l in range(h):
        value = jnp.zeros((owned, every), jnp.float32)
        if l == h - 1:
            value = value + jnp.where(side == 1 - me % 2, laid_ends[:, :every], 0.0)
        if l == 0:
            value = value + jnp.where(side == me % 2, laid_ends[:, every:], 0.0)
        if every < LANES:
            value = jnp.concatenate([value, jnp.zeros((owned, LANES - every), jnp.float32)], axis=1)
        for m in range(end_weights.shape[0]):
            end_weights[m, pl.ds(l, owned, stride=h), :] = value[:, tile(m)]
    count = groups * (many // LANES)
    for f in range(ROWS // h):
        both = jnp.concatenate([weights[f * count + m] for m in range(count)], axis=1).astype(jnp.bfloat16)
        table[:, f * core : (f + 1) * core] = dot(both, merged[...])
    both = jnp.concatenate([end_weights[m] for m in range(end_weights.shape[0])], axis=1)[:, :every]
    extra[...] = dot(both.astype(jnp.bfloat16), ends[...])
    lane = lane_iota((rows, LANES))
    low = lane < edge
    after = (lane // edge) * edge + (lane + 1) % edge
    before = (lane // edge) * edge + (lane + edge - 1) % edge

    def cut(slot, j):
        return table[slot * rows : (slot + 1) * rows, tile(j % columns)]

    for j in range(columns):
        turned = swap_halves(jnp.where(low, cut(1, j + 1) + cut(2, j), cut(1, j) + cut(2, j - 1)))
        value = cut(0, j) + extra[:, tile(j)] + turned
        value = value + pick_lanes(cut(3, j), after) + pick_lanes(cut(4, j), before)
        for o in range(owned):
            out_ref[o, :, tile(j)] = value[o * h : (o + 1) * h, :]


def in_vmem():
    return pl.BlockSpec(memory_space=pltpu.VMEM)


def anywhere():
    return pl.BlockSpec(memory_space=pl.ANY)


def per_device(particles, references, orient, allowed):
    edge = particles.shape[1]
    wide = edge * edge
    total = orient.shape[0]
    parts = lax.axis_size("dp")
    groups = lax.axis_size("ref")
    devices = parts * groups
    h = edge // parts
    planes = 2 * h
    rows = total * h
    owned = total // groups
    span = SLOTS * parts
    core_lanes, _, extra = lanes_of(edge, parts)
    payload = sum(lanes_of(edge, parts))
    scale = 3.0 / math.sqrt(edge**3)
    params = pltpu.CompilerParams(vmem_limit_bytes=VMEM_BYTES)
    f32, bf16 = jnp.float32, jnp.bfloat16
    array = jax.ShapeDtypeStruct
    turning = [
        pltpu.VMEM((ROWS, wide), f32),
        pltpu.VMEM((ROWS, wide), f32),
        pltpu.VMEM((planes * edge, LANES), f32),
        pltpu.VMEM((planes * edge, LANES), f32),
    ]
    far = lax.ppermute(references, "dp", [(i, parts - 1 - i) for i in range(parts)])
    sent, both = pl.pallas_call(
        functools.partial(pack_kernel, edge, parts),
        out_shape=(array((parts * ROWS, payload), bf16), array((2 * planes, wide), bf16)),
        in_specs=[anywhere()] * 2,
        out_specs=(in_vmem(), in_vmem()),
        scratch_shapes=[
            pltpu.VMEM((edge, wide), bf16),
            pltpu.VMEM(references.shape, bf16),
            pltpu.SemaphoreType.DMA((1 + edge // (2 * ROWS),)),
            pltpu.VMEM((edge + 2 * ROWS, wide), f32),
            pltpu.VMEM((parts * ROWS, payload), f32),
            *turning,
        ],
        compiler_params=pltpu.CompilerParams(vmem_limit_bytes=MOST_VMEM),
        name="pack",
    )(particles.reshape(edge, wide), references)
    own = pl.pallas_call(
        functools.partial(own_kernel, h, wide // LANES),
        out_shape=array((4 * wide // LANES, ROWS, LANES), f32),
        in_specs=[in_vmem()],
        out_specs=in_vmem(),
        compiler_params=params,
        cost_estimate=pl.CostEstimate(flops=0, bytes_accessed=16 * 1024 * 1024, transcendentals=0),
        name="own",
    )(both)
    got = lax.all_to_all(sent, "dp", 0, 0, tiled=True)
    got, own, far = lax.optimization_barrier((got, own, far))
    plane = array((parts, wide), bf16)
    core, outer, lacking = pl.pallas_call(
        functools.partial(trim_kernel, edge, parts),
        out_shape=(array((parts * ROWS, core_lanes), bf16), plane, plane),
        in_specs=[in_vmem()],
        out_specs=(in_vmem(),) * 3,
        compiler_params=params,
        name="trim",
    )(got)
    pairs = [(i, i ^ 1) for i in range(parts)]
    inner = lax.ppermute(lacking, "dp", pairs)
    steps = [[(i, (i + k) % groups) for i in range(groups)] for k in range(1, groups)]
    cores = [lax.ppermute(core, "ref", step) for step in steps]
    partial, base, bars = pl.pallas_call(
        functools.partial(logits_kernel, edge, parts, total),
        out_shape=(array((total, span), f32), array((rows, wide), bf16), array((total, span), f32)),
        in_specs=[anywhere()] * 2 + [in_vmem()] * 3,
        out_specs=(in_vmem(),) * 3,
        scratch_shapes=[
            pltpu.SMEM(orient.shape, jnp.int32),
            pltpu.SMEM(allowed.shape, jnp.int32),
            pltpu.SemaphoreType.DMA((2,)),
            *turning,
            pltpu.VMEM((extra // LANES, parts * ROWS, LANES), f32),
            pltpu.VMEM((2, planes * edge, LANES), f32),
            pltpu.VMEM((2, planes * edge, LANES), f32),
            pltpu.VMEM((24 * wide // LANES, ROWS, LANES), f32),
            pltpu.VMEM((len(FLAT) * rows, wide), bf16),
            pltpu.VMEM((len(FLAT) * rows, parts * ROWS), f32),
        ],
        compiler_params=params,
        name="logits",
    )(orient, allowed, got, own, far)
    partial = pl.pallas_call(
        functools.partial(finish_kernel, h, parts, devices, scale),
        out_shape=array((devices * total, span), f32),
        in_specs=[in_vmem()] * 5,
        out_specs=in_vmem(),
        scratch_shapes=[pltpu.VMEM((rows, LANES), f32)],
        compiler_params=params,
        name="finish",
    )(partial, base, bars, outer, inner)
    partial, outside = lax.optimization_barrier((partial, outer))
    logits = lax.all_to_all(partial, ("ref", "dp"), 0, 0, tiled=True)
    tables = [array((span, len(MOVES) * parts * ROWS), bf16)]
    pieces = [outer, inner]
    for core, step in zip(cores, steps, strict=True):
        lacking, *laid = pl.pallas_call(
            functools.partial(far_ends_kernel, h),
            out_shape=(plane, *tables),
            in_specs=[in_vmem()],
            out_specs=(in_vmem(),) * (1 + len(tables)),
            compiler_params=params,
            cost_estimate=pl.CostEstimate(flops=0, bytes_accessed=16 * 1024 * 1024, transcendentals=0),
            name="far_ends",
        )(core)
        spread = laid[0] if laid else spread
        pieces += [core, lax.ppermute(outside, "ref", step), lax.ppermute(lacking, "dp", pairs)]
        tables = []
    every = groups * 2 * parts
    sums, log_evidence = pl.pallas_call(
        functools.partial(sums_kernel, edge, parts, total, groups),
        out_shape=(array((owned, h, wide), f32), array((1, 1), f32)),
        in_specs=[in_vmem()] * (3 + len(pieces)),
        out_specs=(in_vmem(), in_vmem()),
        scratch_shapes=[
            pltpu.VMEM((groups, total, span), f32),
            pltpu.VMEM((ROWS // h * groups * parts * ROWS // LANES, len(FLAT) * owned * h, LANES), f32),
            pltpu.VMEM((max(every // LANES, 1), owned * h, LANES), f32),
            pltpu.VMEM((len(FLAT) * owned * h, wide), f32),
            pltpu.VMEM((owned * h, wide), f32),
            pltpu.VMEM((groups * parts * ROWS, core_lanes), bf16),
            pltpu.VMEM((every, wide), bf16),
        ],
        compiler_params=params,
        name="sums",
    )(logits, spread, got, *pieces)
    return (sums, log_evidence.reshape(1))


def solution(mesh):
    return jax.shard_map(
        per_device,
        mesh=mesh,
        in_specs=(P(("ref", "dp"), None, None), P(None, "dp", None), P(), P(("ref", "dp"), None)),
        out_specs=(P("ref", "dp", None), P(("ref", "dp"))),
        check_vma=False,
    )
```

```python
import functools
import math

import jax
import jax.numpy as jnp
from jax import lax
from jax.experimental import pallas as pl
from jax.experimental.pallas import tpu as pltpu
from jax.sharding import PartitionSpec as P

ORI = 8
LANES = 128
ROWS = 8
MOVES = [(0, 0, 0), (1, 0, 0), (-1, 0, 0), (0, 1, 0), (0, -1, 0), (0, 0, 1), (0, 0, -1)]
FLAT = [(0, 0), (1, 0), (-1, 0), (0, 1), (0, -1)]
SLOTS = 8
BARRED = -1e30
VMEM_BYTES = 24 * 1024 * 1024
MOST_VMEM = 62 * 1024 * 1024


def lane_iota(shape):
    return lax.broadcasted_iota(jnp.int32, shape, len(shape) - 1)


def row_iota(shape):
    return lax.broadcasted_iota(jnp.int32, shape, 0)


def swap_halves(x):
    return pltpu.roll(x, LANES // 2, 1)


def rows_by_rows(a, b):
    return lax.dot_general(a, b, (((1,), (1,)), ((), ())), preferred_element_type=jnp.float32)


def pick_lanes(x, index):
    return jnp.take_along_axis(x, index, axis=1, mode="promise_in_bounds")


def tile(m):
    return slice(m * LANES, (m + 1) * LANES)


def lanes_of(edge, parts):
    h = edge // parts
    return edge * edge * h // ROWS, 4 * h * edge


def turn_rows(edge, planes, x, z, flat, turned):
    lay_rows(edge, planes, x, flat)
    turn_planes(edge, planes, flat, turned)
    gather_rows(edge, planes, turned, z)


def lay_rows(edge, planes, x, flat):
    for m in range(edge // 2):
        piece = x[:planes, tile(m)]
        flat[pl.ds(2 * m, planes, stride=edge), :] = piece
        flat[pl.ds(2 * m + 1, planes, stride=edge), :] = swap_halves(piece)


def turn_planes(edge, planes, flat, turned):
    for n in range(0, planes, 2):
        block = flat[n * edge : (n + 2) * edge, :].T[:edge, :]
        turned[n * edge : (n + 1) * edge, :] = block
        turned[(n + 1) * edge : (n + 2) * edge, :] = swap_halves(block)


def gather_rows(edge, planes, turned, z):
    low = lane_iota((planes, LANES)) < edge
    for m in range(edge // 2):
        even = turned[pl.ds(2 * m, planes, stride=edge), :]
        odd = turned[pl.ds(2 * m + 1, planes, stride=edge), :]
        z[:planes, tile(m)] = jnp.where(low, even, swap_halves(odd))


def pack_kernel(
    edge, parts, part_hbm, refs_hbm, out_ref, both_ref, part_ref, refs_ref, sems, ring, stage, x, z, flat, turned
):
    h = edge // parts
    planes = 2 * h
    core, _ = lanes_of(edge, parts)
    chunk = 2 * ROWS
    refs_copy = pltpu.make_async_copy(refs_hbm, refs_ref, sems.at[0])
    refs_copy.start()
    copies = []
    for i in range(edge // chunk):
        rows = pl.ds(i * chunk, chunk)
        copies.append(pltpu.make_async_copy(part_hbm.at[rows], part_ref.at[rows], sems.at[1 + i]))
        copies[-1].start()
    refs_copy.wait()
    for c in range(2):
        x[c * h : (c + 1) * h, :] = refs_ref[c].astype(jnp.float32)
    turn_rows(edge, planes, x, z, flat, turned)
    both_ref[...] = jnp.concatenate([x[:planes, :], z[:planes, :]], axis=0).astype(jnp.bfloat16)
    if planes < ROWS:
        stage[...] = jnp.zeros_like(stage)
    slab = h * edge
    for s in range(parts):
        top = s * ROWS
        mirror = parts - 1 - s
        for number, (array, place) in enumerate(((x, s), (x, mirror), (z, s), (z, mirror))):
            left = core + number * slab
            stage[top : top + planes, left : left + slab] = array[:planes, place * slab : (place + 1) * slab]
    last = len(copies) - 1
    done = 0
    for i in [last] + list(range(last)):
        copies[i].wait()
        rows = slice(i * chunk, (i + 1) * chunk)
        ring[ROWS + i * chunk : ROWS + (i + 1) * chunk, :] = part_ref[rows, :].astype(jnp.float32)
        if i == last:
            ring[ROWS - 1 : ROWS, :] = ring[ROWS + edge - 1 : ROWS + edge, :]
        if i == 0:
            ring[ROWS + edge : ROWS + edge + 1, :] = ring[ROWS : ROWS + 1, :]
        ready = 0 if i == last else (parts if i == last - 1 else ((i + 1) * chunk - 1) // h)
        while done + 2 <= ready:
            for s in (done, done + 1):
                top, first = s * ROWS, ROWS + h * s
                for f in range(ROWS // h):
                    stage[top + f * h : top + (f + 1) * h, :core] = ring[first : first + h, f * core : (f + 1) * core]
            both = slice(done * ROWS, (done + 2) * ROWS)
            out_ref[both, :] = stage[both, :].astype(jnp.bfloat16)
            done += 2


def own_kernel(h, columns, parts, allowed_ref, both_ref, out_ref, bar_ref):
    planes = 2 * h
    own = both_ref[...].astype(jnp.float32)
    for turn in range(2):
        for c in range(2):
            top = turn * planes + c * h
            for copy in range(ROWS // h):
                for m in range(columns):
                    out_ref[(turn * 2 + c) * columns + m, copy * h : (copy + 1) * h, :] = own[top : top + h, tile(m)]
    kin = row_iota(bar_ref.shape) // ORI
    permit = jnp.zeros(bar_ref.shape, jnp.int32)
    for c in range(bar_ref.shape[0] // ORI):
        permit = jnp.where(kin == c, allowed_ref[0, c], permit)
    barred = (lane_iota(bar_ref.shape) % parts == lax.axis_index("dp")) & (permit != 1)
    bar_ref[...] = jnp.where(barred, jnp.float32(BARRED), jnp.float32(0.0))


def logits_kernel(
    edge, parts, total, orient_any, got_ref, own_ref, far_ref, out_ref, base_ref,
    orient_ref, sem, x, z, far_flat, far_turned, wide_f32, flats, turneds, kinds, shifted, gram,
):
    h = edge // parts
    wide = edge * edge
    columns = wide // LANES
    rows = total * h
    core, extra = lanes_of(edge, parts)
    planes = 2 * h
    scalars = pltpu.make_async_copy(orient_any, orient_ref, sem)
    scalars.start()
    low = lane_iota((ROWS, LANES)) < edge
    for j in range(extra // LANES):
        wide_f32[j] = got_ref[:, tile(core // LANES + j)].astype(jnp.float32)

    def keep(first, second, value, m):
        if planes == ROWS:
            upper = row_iota((ROWS, LANES)) < h
            other = pltpu.roll(value, h, 0)
            kinds[first * columns + m] = jnp.where(upper, value, other)
            kinds[second * columns + m] = jnp.where(upper, other, value)
        else:
            for number, kind in enumerate((first, second)):
                for copy in range(ROWS // h):
                    kinds[kind * columns + m, copy * h : (copy + 1) * h, :] = value[number * h : (number + 1) * h, :]

    for turn in range(2):
        for c in range(2):
            source, target = (turn * 2 + c) * columns, (turn * 4 + c) * columns
            kinds[target : target + columns] = own_ref[source : source + columns]
    for c in range(2):
        far = far_ref[c].astype(jnp.float32)
        for l in range(h):
            x[c * h + l : c * h + l + 1, :] = far[h - 1 - l : h - l, :]
    lay_rows(edge, planes, x, far_flat)
    for axis in (1, 2):
        flat = flats.at[axis - 1]
        for c in range(2):
            for jl in range(h):
                first = (axis - 1) * 2 * h * edge // LANES
                for s in range(0, parts, ROWS):
                    tiles = [
                        wide_f32[first + i, pl.ds(s * ROWS + c * h + jl, ROWS, stride=ROWS), :] for i in range(h)
                    ]
                    for l in range(h):
                        plain, mirrored = tiles[l // 2], tiles[h // 2 + (h - 1 - l) // 2]
                        if l % 2 == 0:
                            value = jnp.where(low, plain, mirrored)
                        else:
                            value = swap_halves(jnp.where(low, mirrored, plain))
                        flat[pl.ds((c * h + l) * edge + s * h + jl, ROWS, stride=h), :] = value
    turn_planes(edge, planes, far_flat, far_turned)
    for axis in (1, 2):
        flat, turned = flats.at[axis - 1], turneds.at[axis - 1]
        for l in range(h):
            block = jnp.concatenate(
                [flat[(c * h + l) * edge : (c * h + l + 1) * edge, :] for c in range(2)], axis=0
            ).T
            for side in range(2):
                turned[(side * h + l) * edge : (side * h + l + 1) * edge, :] = block[side * edge : (side + 1) * edge, :]
    gather_rows(edge, planes, far_turned, z)
    for m in range(columns):
        keep(2, 3, x[:planes, tile(m)], m)
        keep(6, 7, z[:planes, tile(m)], m)
    for axis in (1, 2):
        flat, turned = flats.at[axis - 1], turneds.at[axis - 1]
        part = lane_iota((planes, LANES)) < edge
        for m in range(edge // 2):
            even = flat[pl.ds(2 * m, planes, stride=edge), :]
            odd = flat[pl.ds(2 * m + 1, planes, stride=edge), :]
            keep(axis * 8, axis * 8 + 1, jnp.where(part, even, swap_halves(odd)), m)
            keep(axis * 8 + 2, axis * 8 + 3, jnp.where(part, swap_halves(even), odd), m)
            even = turned[pl.ds(2 * m, planes, stride=edge), :]
            odd = turned[pl.ds(2 * m + 1, planes, stride=edge), :]
            keep(axis * 8 + 4, axis * 8 + 6, jnp.where(part, even, swap_halves(odd)), m)
            keep(axis * 8 + 5, axis * 8 + 7, jnp.where(part, swap_halves(even), odd), m)
    scalars.wait()
    lane = lane_iota((ROWS, LANES))
    slot = row_iota((ROWS, LANES)) // h
    per = ROWS // h
    lows = lane < edge
    after = (lane // edge) * edge + (lane + 1) % edge
    before = (lane // edge) * edge + (lane + edge - 1) % edge
    start, step, index = [], [], []
    for b in range(total // per):
        xor = jnp.zeros((ROWS, LANES), jnp.int32)
        for i in range(per):
            o = b * per + i
            turn = (orient_ref[o, 1] > orient_ref[o, 2]).astype(jnp.int32)
            kind = orient_ref[o, 0] * 8 + turn * 4 + orient_ref[o, 3] * 2 + o // ORI
            start.append(kind * columns + orient_ref[o, 4] * (columns - 1))
            step.append(1 - 2 * orient_ref[o, 4])
            xor = jnp.where(slot == i, orient_ref[o, 4] * edge + orient_ref[o, 5] * (edge - 1), xor)
        index.append([lane ^ xor, (lane ^ edge) ^ xor, before ^ xor, after ^ xor])

    def piece(o, j):
        return kinds[start[o] + j * step[o]]

    def column(j):
        found = []
        for b in range(total // per):
            value = piece(b * per, j)
            for i in range(1, per):
                value = jnp.where(slot == i, piece(b * per + i, j), value)
            found.append([pick_lanes(value, way) for way in index[b]])
        return [list(way) for way in zip(*found, strict=True)]

    many = parts * ROWS
    fraction = lane_iota((len(FLAT) * rows, many)) % ROWS // h
    blocks = []

    def put(number, j, result):
        at = j % columns
        shifted[number * rows : (number + 1) * rows, tile(at)] = result
        if number == 0:
            base_ref[:, tile(at)] = result

    def joined(result):
        return jnp.concatenate(result, axis=0).astype(jnp.bfloat16)

    def between(first, second):
        return joined([jnp.where(lows, x, y) for x, y in zip(first[1], second[1], strict=True)])

    here = column(0)
    put(1, 0, between(column(columns - 1), here))
    for j in range(columns):
        ahead = column((j + 1) % columns)
        put(0, j, joined(here[0]))
        put(3, j, joined(here[2]))
        put(4, j, joined(here[3]))
        middle = between(here, ahead)
        put(2, j, middle)
        if j + 1 < columns:
            put(1, j + 1, middle)
        here = ahead
        f, rest = divmod((j + 1) * LANES, core)
        if rest == 0:
            blocks.append(rows_by_rows(shifted[:, (f - 1) * core : f * core], got_ref[:, :core]))
    found = blocks[0]
    for f in range(1, ROWS // h):
        found = jnp.where(fraction == f, blocks[f], found)
    gram[...] = found
    place = lane_iota((total, many)) % h
    kept = []
    for t, move in enumerate(MOVES):
        source = FLAT.index((move[1], move[2]))
        total_t = None
        for l in range(h):
            if many == LANES:
                block = gram[pl.ds(source * rows + l, total, stride=h), :]
            else:
                block = jnp.concatenate(
                    [gram[source * rows + o * h + l : source * rows + o * h + l + 1, :] for o in range(total)], axis=0
                )
            block = jnp.where(place == l + move[0], block, 0.0)
            total_t = block if total_t is None else total_t + block
        kept.append(total_t)
    if many == LANES:
        lane = lane_iota((total, LANES))
        result = jnp.zeros((total, LANES), jnp.float32)
        for t in range(len(MOVES)):
            value = kept[t]
            for step in (1, 2, 4):
                value = value + pltpu.roll(value, LANES - step, 1)
            result = jnp.where(lane // parts == t, pick_lanes(value, (lane % parts) * ROWS), result)
    else:
        shape = (len(MOVES) * many, SLOTS * parts)
        picker = (row_iota(shape) // ROWS == lane_iota(shape)).astype(jnp.float32)
        result = exactly(jnp.concatenate(kept, axis=1), picker)
    out_ref[...] = result


def exactly(a, b):
    return jnp.dot(a, b, preferred_element_type=jnp.float32, precision=lax.Precision.HIGHEST)


def finish_kernel(
    h, parts, devices, scale, part_ref, base_ref, bar_ref, outer_ref, inner_ref, out_ref, ends
):
    me = lax.axis_index("dp")
    total = part_ref.shape[0]
    ends[:, : 2 * parts] = rows_by_rows(base_ref[...], jnp.concatenate([outer_ref[...], inner_ref[...]], axis=0))
    beyond = {1: (h - 1, parts * (1 - me % 2)), -1: (0, parts * (me % 2))}
    result = part_ref[...]
    lane = lane_iota(result.shape)
    for t, move in enumerate(MOVES):
        if not move[0]:
            continue
        l, left = beyond[move[0]]
        if result.shape[1] == LANES:
            value = pick_lanes(ends[pl.ds(l, total, stride=h), :], lane % parts + left)
            result = result + jnp.where(lane // parts == t, value, 0.0)
        else:
            shape = (2 * parts, SLOTS * parts)
            block = jnp.concatenate([ends[o * h + l : o * h + l + 1, : 2 * parts] for o in range(total)], axis=0)
            chosen = (row_iota(shape) == lane_iota(shape) % parts + left) & (lane_iota(shape) // parts == t)
            result = result + exactly(block, chosen.astype(jnp.float32))
    result = result * scale
    result = result + bar_ref[...]
    for d in range(devices):
        out_ref[d * total : (d + 1) * total, :] = result


def trim_kernel(edge, parts, got_ref, core_ref, *lacking):
    h = edge // parts
    core, _ = lanes_of(edge, parts)
    core_ref[...] = got_ref[:, :core]
    whole = got_ref[:, :core].reshape(parts, ROWS, core)
    for last_if, ref in enumerate(lacking):
        own_end(h, whole, last_if, ref)


def own_end(h, whole, last_if, out_ref):
    core = whole.shape[2]
    last = lax.axis_index("dp") % 2 == last_if

    @pl.when(last)
    def _():
        for f in range(ROWS // h):
            out_ref[:, f * core : (f + 1) * core] = whole[:, f * h + h - 1, :]

    @pl.when(jnp.logical_not(last))
    def _():
        for f in range(ROWS // h):
            out_ref[:, f * core : (f + 1) * core] = whole[:, f * h, :]


def far_ends_kernel(h, core_ref, out_ref, *tables):
    parts = core_ref.shape[0] // ROWS
    own_end(h, core_ref[...].reshape(parts, ROWS, core_ref.shape[1]), 0, out_ref)
    for table in tables:
        many = parts * ROWS
        column = lane_iota(table.shape)
        particle = column % many // ROWS
        table[...] = (column // many * parts + particle == row_iota(table.shape)).astype(table.dtype)


def sums_kernel(edge, parts, total, groups, logits_ref, spread_ref, got_ref, *refs):
    pieces, refs = refs[: 3 * groups - 1], refs[3 * groups - 1 :]
    out_ref, log_ref, chances, weights, end_weights, table, extra, merged, ends = refs
    h = edge // parts
    wide = edge * edge
    columns = wide // LANES
    owned = total // groups
    rows = owned * h
    span = SLOTS * parts
    many = parts * ROWS
    core, _ = lanes_of(edge, parts)
    mine, me = lax.axis_index("ref"), lax.axis_index("dp")
    at_core, at_end = many, 0
    for piece in pieces:
        if piece.shape[0] == many:
            merged[at_core : at_core + many, :] = piece[...]
            at_core += many
        else:
            ends[at_end : at_end + parts, :] = piece[...]
            at_end += parts
    merged[:many, :] = got_ref[:, :core]
    dot = functools.partial(jnp.dot, preferred_element_type=jnp.float32)
    lane = lane_iota((total, span))
    log_evidence = jnp.zeros((1, span), jnp.float32)
    for g in range(groups):
        scores = [logits_ref[(g * parts + s) * total : (g * parts + s + 1) * total, :] for s in range(parts)]
        while len(scores) > 1:
            scores = [sum(scores[i : i + 2]) for i in range(0, len(scores), 2)]
        score = jnp.where(lane >= len(MOVES) * parts, jnp.float32(-3e38), scores[0])
        peak = jnp.max(score, axis=0, keepdims=True)
        for step in (1, 2, 4):
            peak = jnp.maximum(peak, pltpu.roll(peak, step * parts, 1))
        expo = jnp.exp(score - peak)
        mass = jnp.sum(expo, axis=0, keepdims=True)
        for step in (1, 2, 4):
            mass = mass + pltpu.roll(mass, step * parts, 1)
        chances[g] = expo / mass
        log_evidence = jnp.where(mine == g, peak + jnp.log(mass), log_evidence)
    log_ref[...] = jnp.sum(jnp.where(lane_iota((1, span)) == me, log_evidence, 0.0), axis=1, keepdims=True)
    every = ends.shape[0]
    place, fraction = lane_iota((owned, many)) % h, lane_iota((owned, many)) % ROWS // h
    laid_ends = jnp.zeros((owned, 2 * every), jnp.float32)
    for k in range(groups):
        g = lax.rem(mine + groups - k, groups)
        if owned % ROWS == 0:
            chosen = chances[g, pl.ds(pl.multiple_of(mine * owned, ROWS), owned), :].astype(jnp.bfloat16)
        else:
            at = mine * owned + row_iota((owned, total))
            chooser = (at == lane_iota((owned, total))).astype(jnp.bfloat16)
            chosen = dot(chooser, chances[g].astype(jnp.bfloat16)).astype(jnp.bfloat16)
        laid = dot(chosen, spread_ref[...])
        for slot in range(len(FLAT)):
            for l in range(h):
                value = jnp.zeros((owned, many), jnp.float32)
                for t, move in enumerate(MOVES):
                    if FLAT.index((move[1], move[2])) == slot:
                        value = jnp.where(place == l + move[0], laid[:, t * many : (t + 1) * many], value)
                for f in range(ROWS // h):
                    part = jnp.where(fraction == f, value, 0.0)
                    for m in range(many // LANES):
                        at = (f * groups + k) * (many // LANES) + m
                        weights[at, pl.ds(slot * rows + l, owned, stride=h), :] = part[:, tile(m)]
        shape = (span, 2 * every)
        column = lane_iota(shape)
        up, down = MOVES.index((1, 0, 0)), MOVES.index((-1, 0, 0))
        shift = jnp.where(column < every, up, down)
        here = (column % every // (2 * parts) == k) & (row_iota(shape) == shift * parts + column % parts)
        laid_ends = laid_ends + dot(chosen, here.astype(jnp.bfloat16))
    side = lane_iota((owned, every)) % (2 * parts) // parts
    for l in range(h):
        value = jnp.zeros((owned, every), jnp.float32)
        if l == h - 1:
            value = value + jnp.where(side == 1 - me % 2, laid_ends[:, :every], 0.0)
        if l == 0:
            value = value + jnp.where(side == me % 2, laid_ends[:, every:], 0.0)
        if every < LANES:
            value = jnp.concatenate([value, jnp.zeros((owned, LANES - every), jnp.float32)], axis=1)
        for m in range(end_weights.shape[0]):
            end_weights[m, pl.ds(l, owned, stride=h), :] = value[:, tile(m)]
    count = groups * (many // LANES)
    for f in range(ROWS // h):
        both = jnp.concatenate([weights[f * count + m] for m in range(count)], axis=1).astype(jnp.bfloat16)
        table[:, f * core : (f + 1) * core] = dot(both, merged[...])
    both = jnp.concatenate([end_weights[m] for m in range(end_weights.shape[0])], axis=1)[:, :every]
    extra[...] = dot(both.astype(jnp.bfloat16), ends[...])
    lane = lane_iota((rows, LANES))
    low = lane < edge
    after = (lane // edge) * edge + (lane + 1) % edge
    before = (lane // edge) * edge + (lane + edge - 1) % edge

    def cut(slot, j):
        return table[slot * rows : (slot + 1) * rows, tile(j % columns)]

    for j in range(columns):
        turned = swap_halves(jnp.where(low, cut(1, j + 1) + cut(2, j), cut(1, j) + cut(2, j - 1)))
        value = cut(0, j) + extra[:, tile(j)] + turned
        value = value + pick_lanes(cut(3, j), after) + pick_lanes(cut(4, j), before)
        for o in range(owned):
            out_ref[o, :, tile(j)] = value[o * h : (o + 1) * h, :]


def in_vmem():
    return pl.BlockSpec(memory_space=pltpu.VMEM)


def anywhere():
    return pl.BlockSpec(memory_space=pl.ANY)


def per_device(particles, references, orient, allowed):
    edge = particles.shape[1]
    wide = edge * edge
    total = orient.shape[0]
    parts = lax.axis_size("dp")
    groups = lax.axis_size("ref")
    devices = parts * groups
    h = edge // parts
    planes = 2 * h
    rows = total * h
    owned = total // groups
    span = SLOTS * parts
    core_lanes, extra = lanes_of(edge, parts)
    payload = sum(lanes_of(edge, parts))
    scale = 3.0 / math.sqrt(edge**3)
    params = pltpu.CompilerParams(vmem_limit_bytes=VMEM_BYTES)
    f32, bf16 = jnp.float32, jnp.bfloat16
    array = jax.ShapeDtypeStruct
    turning = [
        pltpu.VMEM((ROWS, wide), f32),
        pltpu.VMEM((ROWS, wide), f32),
        pltpu.VMEM((planes * edge, LANES), f32),
        pltpu.VMEM((planes * edge, LANES), f32),
    ]
    far = lax.ppermute(references, "dp", [(i, parts - 1 - i) for i in range(parts)])
    sent, both = pl.pallas_call(
        functools.partial(pack_kernel, edge, parts),
        out_shape=(array((parts * ROWS, payload), bf16), array((2 * planes, wide), bf16)),
        in_specs=[anywhere()] * 2,
        out_specs=(in_vmem(), in_vmem()),
        scratch_shapes=[
            pltpu.VMEM((edge, wide), bf16),
            pltpu.VMEM(references.shape, bf16),
            pltpu.SemaphoreType.DMA((1 + edge // (2 * ROWS),)),
            pltpu.VMEM((edge + 2 * ROWS, wide), f32),
            pltpu.VMEM((parts * ROWS, payload), f32),
            *turning,
        ],
        compiler_params=pltpu.CompilerParams(vmem_limit_bytes=MOST_VMEM),
        name="pack",
    )(particles.reshape(edge, wide), references)
    own, bars = pl.pallas_call(
        functools.partial(own_kernel, h, wide // LANES, parts),
        out_shape=(array((4 * wide // LANES, ROWS, LANES), f32), array((total, span), f32)),
        in_specs=[pl.BlockSpec(memory_space=pltpu.SMEM), in_vmem()],
        out_specs=(in_vmem(), in_vmem()),
        compiler_params=params,
        cost_estimate=pl.CostEstimate(flops=0, bytes_accessed=16 * 1024 * 1024, transcendentals=0),
        name="own",
    )(allowed, both)
    got = lax.all_to_all(sent, "dp", 0, 0, tiled=True)
    got, own, bars, far = lax.optimization_barrier((got, own, bars, far))
    plane = array((parts, wide), bf16)
    core, lacking, beyond = pl.pallas_call(
        functools.partial(trim_kernel, edge, parts),
        out_shape=(array((parts * ROWS, core_lanes), bf16), plane, plane),
        in_specs=[in_vmem()],
        out_specs=(in_vmem(),) * 3,
        compiler_params=params,
        name="trim",
    )(got)
    pairs = [(i, i ^ 1) for i in range(parts)]
    across = [(i, (i + 1 if i % 2 else i - 1) % parts) for i in range(parts)]
    outer = lax.ppermute(beyond, "dp", across)
    inner = lax.ppermute(lacking, "dp", pairs)
    steps = [[(i, (i + k) % groups) for i in range(groups)] for k in range(1, groups)]
    cores = [lax.ppermute(core, "ref", step) for step in steps]
    partial, base = pl.pallas_call(
        functools.partial(logits_kernel, edge, parts, total),
        out_shape=(array((total, span), f32), array((rows, wide), bf16)),
        in_specs=[anywhere()] + [in_vmem()] * 3,
        out_specs=(in_vmem(),) * 2,
        scratch_shapes=[
            pltpu.SMEM(orient.shape, jnp.int32),
            pltpu.SemaphoreType.DMA,
            *turning,
            pltpu.VMEM((extra // LANES, parts * ROWS, LANES), f32),
            pltpu.VMEM((2, planes * edge, LANES), f32),
            pltpu.VMEM((2, planes * edge, LANES), f32),
            pltpu.VMEM((24 * wide // LANES, ROWS, LANES), f32),
            pltpu.VMEM((len(FLAT) * rows, wide), bf16),
            pltpu.VMEM((len(FLAT) * rows, parts * ROWS), f32),
        ],
        compiler_params=params,
        name="logits",
    )(orient, got, own, far)
    partial = pl.pallas_call(
        functools.partial(finish_kernel, h, parts, devices, scale),
        out_shape=array((devices * total, span), f32),
        in_specs=[in_vmem()] * 5,
        out_specs=in_vmem(),
        scratch_shapes=[pltpu.VMEM((rows, LANES), f32)],
        compiler_params=params,
        name="finish",
    )(partial, base, bars, outer, inner)
    partial, outside = lax.optimization_barrier((partial, outer))
    logits = lax.all_to_all(partial, ("ref", "dp"), 0, 0, tiled=True)
    tables = [array((span, len(MOVES) * parts * ROWS), bf16)]
    pieces = [outer, inner]
    for core, step in zip(cores, steps, strict=True):
        lacking, *laid = pl.pallas_call(
            functools.partial(far_ends_kernel, h),
            out_shape=(plane, *tables),
            in_specs=[in_vmem()],
            out_specs=(in_vmem(),) * (1 + len(tables)),
            compiler_params=params,
            cost_estimate=pl.CostEstimate(flops=0, bytes_accessed=16 * 1024 * 1024, transcendentals=0),
            name="far_ends",
        )(core)
        spread = laid[0] if laid else spread
        pieces += [core, lax.ppermute(outside, "ref", step), lax.ppermute(lacking, "dp", pairs)]
        tables = []
    every = groups * 2 * parts
    sums, log_evidence = pl.pallas_call(
        functools.partial(sums_kernel, edge, parts, total, groups),
        out_shape=(array((owned, h, wide), f32), array((1, 1), f32)),
        in_specs=[in_vmem()] * (3 + len(pieces)),
        out_specs=(in_vmem(), in_vmem()),
        scratch_shapes=[
            pltpu.VMEM((groups, total, span), f32),
            pltpu.VMEM((ROWS // h * groups * parts * ROWS // LANES, len(FLAT) * owned * h, LANES), f32),
            pltpu.VMEM((max(every // LANES, 1), owned * h, LANES), f32),
            pltpu.VMEM((len(FLAT) * owned * h, wide), f32),
            pltpu.VMEM((owned * h, wide), f32),
            pltpu.VMEM((groups * parts * ROWS, core_lanes), bf16),
            pltpu.VMEM((every, wide), bf16),
        ],
        compiler_params=params,
        name="sums",
    )(logits, spread, got, *pieces)
    return (sums, log_evidence.reshape(1))


def solution(mesh):
    return jax.shard_map(
        per_device,
        mesh=mesh,
        in_specs=(P(("ref", "dp"), None, None), P(None, "dp", None), P(), P(("ref", "dp"), None)),
        out_specs=(P("ref", "dp", None), P(("ref", "dp"))),
        check_vma=False,
    )
```
